128 devices in a mesh: var: 32 (over z, y, core), lat: 2 (over x_lo), lon: 2 (over x_hi).
Axes of the slice: x: 4 (x_hi: 2, x_lo: 2; x = x_hi * 2 + x_lo), y: 4, z: 4, core: 2. Of those that a mesh axis runs over, the one named last changes fastest.
Arguments:
- pixels: bfloat16 [32, 24, 64, 4, 384], P(None, 'lat', 'var', None, 'lon'), may hold values from -6 to 6
- var_order: int32 [64], replicated, may hold values from 0 to 63, each once
- embed_weight: bfloat16 [64, 16, 512], P('var'), may hold values from -0.1875 to 0.1875
- level_mix: float32 [64, 2], replicated, may hold values from -3 to 3
- norm_gain: float32 [512], replicated, may hold values from 0.5 to 1.5
- w_qkv: bfloat16 [512, 1536], replicated, may hold values from -4 to 4
- w_proj: bfloat16 [512, 512], replicated, may hold values from -0.25 to 0.25
- mask_ids: int32 [768, 2, 96], P(('var', 'lat'), None, 'lon'), may hold values from 0 to 2
- cotangent: bfloat16 [768, 2, 96, 512], P(('var', 'lat'), None, 'lon'), may hold values from -0.015625 to 0.015625
Outputs:
- block_out: bfloat16 [768, 2, 96, 512], P(('var', 'lat'), None, 'lon')
- grad_embed: float32 [64, 16, 512], P('var')
- grad_qkv: float32 [512, 1536], replicated
- grad_proj: float32 [512, 512], replicated
The draws below stay inside these ranges and needn't reach their ends.
All inputs are finite; a program needn't handle non-finite values.
Results may differ from the reference program's by a relative error of at most 0.023.
Values may be sent and summed in bfloat16 or wider, within the bound.
No kernel may reach another device: no remote copies, remote signals or barrier semaphores. Data moves between devices by JAX's collectives and lax.ppermute only.
A program may use at most 128 MiB of HBM per device.

```python
import math
import jax
import jax.numpy as jnp
from jax import lax

D = 512
HEADS = 8
HDIM = 64
PSIDE = 4
CHANNELS = 64
LT = 2
ROWS = 12
WCOL = 6
NROWS = 768
COLS = 96
N_VAR = 32
N_LAT = 2


def draw_w_qkv(key, part):
    key = jax.random.fold_in(key, 7)
    base_key = jax.random.fold_in(key, 0)
    standard = jax.random.truncated_normal(base_key, -4.0, 4.0, (D, 3 * D), jnp.float32) / math.sqrt(D)
    return standard.astype(jnp.bfloat16)


def with_ends(drawn, key, low, high):
    longest = drawn.shape.index(max(drawn.shape))
    spots = []
    for shift in (0, 1):
        where = [jax.random.randint(jax.random.fold_in(key, axis), (), 0, length) for axis, length in enumerate(drawn.shape)]
        where[longest] = (where[longest] + shift) % drawn.shape[longest]
        spots.append(tuple(where))
    return drawn.at[spots[0]].set(low).at[spots[1]].set(high)


def shard_levels(key, shape, cuts, low, high):
    level, own = 1.0, jax.random.fold_in(key, 6)
    for dim, blocks in cuts:
        heights = jnp.exp(jax.random.uniform(jax.random.fold_in(own, dim), (blocks,), jnp.float32, low / len(cuts), high / len(cuts)))
        level = level * jnp.repeat(heights, shape[dim] // blocks).reshape([-1 if axis == dim else 1 for axis in range(len(shape))])
    return level


def normal_values(stream_key, extent, scale, bound, cuts=(), dtype=jnp.bfloat16):
    entries = jax.random.normal(stream_key, extent, jnp.float32) * scale
    if len(cuts) > 0:
        entries = shard_levels(stream_key, extent, cuts, -0.22, 0.18) * entries
    return jnp.clip(entries, min=-bound, max=bound).astype(dtype)


def setup_inputs(seed: int = 0) -> dict:
    arg_keys = jax.random.split(jax.random.key(seed), 10)
    pixels = normal_values(arg_keys[0], (N_VAR, N_LAT * ROWS, CHANNELS, PSIDE, COLS * PSIDE), 1.0, 6.0, ((1, 2), (2, 32), (4, 2)))
    var_order = jax.random.permutation(arg_keys[1], CHANNELS).astype(jnp.int32)
    embed_weight = normal_values(arg_keys[2], (CHANNELS, PSIDE * PSIDE, D), (CHANNELS * PSIDE * PSIDE) ** -0.5, 0.1875, ((0, 32),))
    level_mix = normal_values(arg_keys[3], (CHANNELS, LT), 1.0, 3.0, (), jnp.float32)
    norm_gain = jnp.clip(1.0 + 0.1 * jax.random.normal(arg_keys[4], (D,), jnp.float32), 0.5, 1.5)
    w_qkv = draw_w_qkv(jax.random.fold_in(arg_keys[9], 71), 0)
    w_proj = normal_values(arg_keys[6], (D, D), D ** -0.5, 0.25)
    mask_ids = with_ends(jax.random.randint(arg_keys[7], (NROWS, LT, COLS), 0, 3), jax.random.fold_in(arg_keys[7], 1), 0, 2).astype(jnp.int32)
    cotangent = normal_values(arg_keys[8], (NROWS, LT, COLS, D), (NROWS * LT * COLS) ** -0.5, 0.015625, ((0, 64), (2, 2)))
    return {"pixels": pixels, "var_order": var_order, "embed_weight": embed_weight, "level_mix": level_mix, "norm_gain": norm_gain, "w_qkv": w_qkv, "w_proj": w_proj, "mask_ids": mask_ids, "cotangent": cotangent}


epsilon = 1e-05

def rounded(tensor):
    return lax.optimization_barrier(tensor.astype(jnp.bfloat16))

def to_windows(tensor):
    row_count, level_count, col_count, features = tensor.shape
    window_count = col_count // WCOL
    parts = tensor.reshape(row_count, level_count, window_count, WCOL, features)
    return parts.transpose(2, 0, 1, 3, 4).reshape(window_count, row_count * level_count * WCOL, features)

def from_windows(tensor, row_count, level_count):
    window_count, token_count, features = tensor.shape
    parts = tensor.reshape(window_count, row_count, level_count, WCOL, features)
    return parts.transpose(1, 2, 0, 3, 4).reshape(row_count, level_count, window_count * WCOL, features)

def split_heads(windows):
    window_count, token_count = windows.shape[:2]
    parts = windows.reshape(window_count, token_count, 3, HEADS, HDIM)
    return (parts[:, :, 0], parts[:, :, 1], parts[:, :, 2])

def window_probs(query_rows, key_rows, region_ids):
    scores = jnp.einsum('wqhe,wkhe->whqk', query_rows.astype(jnp.float32), key_rows.astype(jnp.float32))
    scores = scores * (1.0 / math.sqrt(HDIM))
    same_region = region_ids[:, None, :, None] == region_ids[:, None, None, :]
    scores = jnp.where(same_region, scores, -1e+30)
    row_max = lax.optimization_barrier(jnp.max(scores, axis=-1, keepdims=True))
    exponent = jnp.exp(scores - row_max)
    return exponent / lax.optimization_barrier(jnp.sum(exponent, axis=-1, keepdims=True))

def attend_block(projected, region_ids):
    row_count, level_count = projected.shape[:2]
    windows = to_windows(projected)
    query_rows, key_rows, value_rows = split_heads(windows)
    attention = window_probs(query_rows, key_rows, to_windows(region_ids[..., None])[..., 0])
    probs_half = rounded(attention).astype(jnp.float32)
    attended = rounded(jnp.einsum('whqk,wkhe->wqhe', probs_half, value_rows.astype(jnp.float32)))
    attended = attended.reshape(windows.shape[0], windows.shape[1], D)
    return from_windows(attended, row_count, level_count)

def attend_back_block(projected, region_ids, grad_attended):
    row_count, level_count = projected.shape[:2]
    windows = to_windows(projected)
    window_count, token_count = windows.shape[:2]
    query_rows, key_rows, value_rows = split_heads(windows)
    attention = window_probs(query_rows, key_rows, to_windows(region_ids[..., None])[..., 0])
    probs_half = rounded(attention).astype(jnp.float32)
    grad_out = to_windows(grad_attended).reshape(window_count, token_count, HEADS, HDIM).astype(jnp.float32)
    grad_value = rounded(jnp.einsum('whqk,wqhe->wkhe', probs_half, grad_out))
    grad_prob = jnp.einsum('wqhe,wkhe->whqk', grad_out, value_rows.astype(jnp.float32))
    centred = grad_prob - lax.optimization_barrier(jnp.sum(attention * grad_prob, axis=-1, keepdims=True))
    grad_score = rounded(attention * centred * (1.0 / math.sqrt(HDIM))).astype(jnp.float32)
    grad_query = rounded(jnp.einsum('whqk,wkhe->wqhe', grad_score, key_rows.astype(jnp.float32)))
    grad_key = rounded(jnp.einsum('whqk,wqhe->wkhe', grad_score, query_rows.astype(jnp.float32)))
    stacked = jnp.stack([grad_query, grad_key, grad_value], axis=2).reshape(window_count, token_count, 3 * D)
    return from_windows(stacked, row_count, level_count)

def layer_norm(tensor, gain):
    values = tensor.astype(jnp.float32)
    average = lax.optimization_barrier(jnp.mean(values, axis=-1, keepdims=True))
    centred = values - average
    inverse_std = lax.rsqrt(lax.optimization_barrier(jnp.mean(centred * centred, axis=-1, keepdims=True)) + epsilon)
    unit_values = centred * inverse_std
    return (rounded(unit_values * gain), unit_values, inverse_std)

def norm_back(grad_normed, unit_values, inverse_std, gain):
    scaled = grad_normed * gain
    return inverse_std * (scaled - lax.optimization_barrier(jnp.mean(scaled, axis=-1, keepdims=True)) - unit_values * lax.optimization_barrier(jnp.mean(scaled * unit_values, axis=-1, keepdims=True)))

def reference(pixels, var_order, embed_weight, level_mix, norm_gain, w_qkv, w_proj, mask_ids, cotangent):
    half_rows = ROWS // 2
    half_cols = WCOL // 2
    pixel_grid = pixels.reshape(NROWS, CHANNELS, PSIDE, COLS, PSIDE).astype(jnp.float32)
    slot_weight = embed_weight[var_order].reshape(CHANNELS, PSIDE, PSIDE, D).astype(jnp.float32)
    slot_mix = level_mix[var_order]
    level_weight = rounded(slot_mix.T[:, :, None, None, None] * slot_weight[None]).astype(jnp.float32)
    tokens = rounded(jnp.einsum('rsacb,lsabd->rlcd', pixel_grid, level_weight))
    shifted = jnp.roll(tokens, (-half_rows, -half_cols), axis=(0, 2))
    normed, unit_values, inverse_std = layer_norm(shifted, norm_gain)
    projected = rounded(jnp.dot(normed.reshape(-1, D), w_qkv, preferred_element_type=jnp.float32))
    projected = projected.reshape(NROWS, LT, COLS, 3 * D)
    block_count = NROWS // ROWS
    proj_blocks = projected.reshape(block_count, ROWS, LT, COLS, 3 * D)
    id_blocks = mask_ids.reshape(block_count, ROWS, LT, COLS)
    attended = lax.map(lambda pair: attend_block(pair[0], pair[1]), (proj_blocks, id_blocks))
    attended = attended.reshape(NROWS * LT * COLS, D)
    branch_out = rounded(jnp.dot(attended, w_proj, preferred_element_type=jnp.float32)).reshape(NROWS, LT, COLS, D)
    block_out = (tokens.astype(jnp.float32) + jnp.roll(branch_out, (half_rows, half_cols), axis=(0, 2)).astype(jnp.float32)).astype(jnp.bfloat16)
    grad_branch = jnp.roll(cotangent, (-half_rows, -half_cols), axis=(0, 2)).reshape(-1, D)
    grad_proj = jnp.dot(attended.T, grad_branch, preferred_element_type=jnp.float32)
    grad_attended = rounded(jnp.dot(grad_branch, w_proj.T, preferred_element_type=jnp.float32))
    grad_blocks = grad_attended.reshape(block_count, ROWS, LT, COLS, D)
    grad_projected = lax.map(lambda trio: attend_back_block(trio[0], trio[1], trio[2]), (proj_blocks, id_blocks, grad_blocks))
    grad_projected = grad_projected.reshape(-1, 3 * D)
    grad_qkv = jnp.dot(normed.reshape(-1, D).T, grad_projected, preferred_element_type=jnp.float32)
    grad_normed = jnp.dot(grad_projected, w_qkv.T, preferred_element_type=jnp.float32).reshape(NROWS, LT, COLS, D)
    grad_shifted = rounded(norm_back(grad_normed, unit_values, inverse_std, norm_gain))
    grad_tokens = rounded(cotangent.astype(jnp.float32) + jnp.roll(grad_shifted, (half_rows, half_cols), axis=(0, 2)).astype(jnp.float32))
    grad_level = jnp.einsum('rsacb,rlcd->lsabd', pixel_grid, grad_tokens.astype(jnp.float32))
    grad_slot = lax.optimization_barrier(jnp.sum(slot_mix.T[:, :, None, None, None] * grad_level, axis=0))
    grad_slot = grad_slot.reshape(CHANNELS, PSIDE * PSIDE, D)
    grad_embed = jnp.zeros((CHANNELS, PSIDE * PSIDE, D), jnp.float32).at[var_order].set(grad_slot)
    return (block_out, grad_embed, grad_qkv, grad_proj)
```

```python
import functools

import jax
import jax.numpy as jnp
import numpy as np
from jax import lax
from jax.experimental import pallas as pl
from jax.experimental.pallas import tpu as pltpu
from jax.sharding import Mesh, PartitionSpec as P

D = 512
HEADS = 8
HDIM = 64
PSIDE = 4
WCOL = 6
ROWS = 12
HALF = 6
COLS = 48
WINDOWS = 8
LEVELS = 2
TOKENS = 1152
WTOK = 144
PATCHES = 576
LANES = 1152
EPS = 1e-05
BF = jnp.bfloat16
F32 = jnp.float32
VMEM_LIMIT = 58 * 1024 * 1024

NN = (((1,), (0,)), ((), ()))
NT = (((1,), (1,)), ((), ()))
TN = (((0,), (0,)), ((), ()))


def dot(a, b, dims=NN):
    return lax.dot_general(a, b, dims, preferred_element_type=F32)


def pixel_lane(b, patch):
    return np.where(patch < 256, 256 * b + patch, 1024 + 32 * b + patch - 256)


def edge_place():
    place = np.zeros((HALF, 128, 128), np.float32)
    for j in range(HALF):
        lane = np.arange(12)
        place[j, lane, j * 12 + lane] = 1
    return place


def pixel_place():
    main = np.zeros((HALF, 4 * COLS, LANES), np.float32)
    edge = np.zeros((128, LANES), np.float32)
    for j in range(HALF):
        for c in range(COLS):
            for b in range(PSIDE):
                col = c - 3 if c >= 3 else COLS - 3 + c
                patch = (col // WCOL) * 36 + j * WCOL + col % WCOL
                lane = pixel_lane(b, patch)
                if c >= 3:
                    main[j, c * PSIDE + b, lane] = 1
                else:
                    edge[j * 12 + c * PSIDE + b, lane] = 1
    return main, edge


def patch_place():
    main = np.zeros((2, PATCHES, 256), np.float32)
    rest = np.zeros((2, PSIDE, PATCHES, 128), np.float32)
    for half in range(2):
        for w in range(WINDOWS):
            for i in range(36):
                patch = w * 36 + i
                row = w * 72 + half * 36 + i
                if patch < 256:
                    main[half, row, patch] = 1
                else:
                    for b in range(PSIDE):
                        rest[half, b, row, 32 * b + patch - 256] = 1
    return main, rest


def token_place():
    place = np.zeros((TOKENS, TOKENS + 128), np.float32)
    for w in range(WINDOWS):
        for level in range(LEVELS):
            for half in range(2):
                for j in range(HALF):
                    for c6 in range(WCOL):
                        t = w * WTOK + level * 72 + half * 36 + j * WCOL + c6
                        c = w * WCOL + c6 + 3
                        if c < COLS:
                            place[t, half * PATCHES + (j * LEVELS + level) * COLS + c] = 1
                        else:
                            place[t, TOKENS + half * 36 + (j * LEVELS + level) * 3 + c - COLS] = 1
    return place


def half_rows(pix_ref, half, j, lanes):
    rows = pix_ref[:, half * HALF + j, :, :, :lanes].astype(F32)
    merged = jnp.concatenate([rows[:, 0], rows[:, 1]], axis=1)
    return merged.reshape(merged.shape[0] * 8, lanes).astype(BF)


def edge_kernel(pix_ref, place_ref, out_ref):
    for half in range(2):
        total = None
        for j in range(HALF):
            term = dot(half_rows(pix_ref, half, j, 128), place_ref[j])
            total = term if total is None else total + term
        out_ref[half] = total.astype(BF)


def pack_kernel(info_ref, pix_ref, main_ref, edge_ref, halo_ref, out_ref):
    lat = info_ref[0]
    bands = out_ref.shape[0]
    for half in range(2):
        total = dot(halo_ref[half], edge_ref[...])
        for j in range(HALF):
            total = total + dot(half_rows(pix_ref, half, j, 4 * COLS), main_ref[j])
        block = total.reshape(bands, 8, LANES).astype(BF)
        if half == 1:
            out_ref[:, lat] = block
        else:

            @pl.when(lat == 0)
            def _():
                out_ref[: bands - 1, 1] = block[1:]
                out_ref[bands - 1 :, 1] = block[:1]

            @pl.when(lat == 1)
            def _():
                out_ref[:, 0] = block


def block_kernel(
    info_ref,
    recv_ref,
    wown_ref,
    woth_ref,
    idxc_ref,
    idxr_ref,
    mix_ref,
    gain_ref,
    wqkv_ref,
    wproj_ref,
    mcol_ref,
    mrow_ref,
    cown_ref,
    cnext_ref,
    cedge_ref,
    pmain_ref,
    prest_ref,
    tok_ref,
    tokt_ref,
    top_ref,
    bot_ref,
    edge_ref,
    gown_ref,
    goth_ref,
    a_s,
    at_s,
    lw_s,
    t_s,
    unit_s,
    inv_s,
    norm_s,
    qkv_s,
    gb_s,
    ga_s,
    att_s,
    gp_s,
    bo_s,
    gt_s,
    gs_s,
):
    lat = info_ref[0]
    core = info_ref[1]
    gain = gain_ref[...]

    halves = []
    for half in range(2):
        src = lat if half == 0 else 1 - lat
        part = recv_ref[:, src].astype(F32)
        halves.append(part.reshape(256, LANES).astype(BF))
    for b in range(PSIDE):
        rows = None
        columns = None
        for half in range(2):
            main = halves[half][:, 256 * b : 256 * b + 256]
            rest = halves[half][:, 1024:1152]
            r = dot(pmain_ref[half], main, NT) + dot(prest_ref[half, b], rest, NT)
            c = dot(main, pmain_ref[half], NT) + dot(rest, prest_ref[half, b], NT)
            rows = r if rows is None else rows + r
            columns = c if columns is None else columns + c
        a_s[:, 256 * b : 256 * b + 256] = rows.astype(BF)
        at_s[256 * b : 256 * b + 256, :] = columns.astype(BF)
        lane = lax.broadcasted_iota(jnp.int32, (256, 512), 1)
        idx = idxc_ref[256 * b : 256 * b + 256, :]
        pick_own = jnp.where(lane == idx, 1.0, 0.0).astype(BF)
        pick_oth = jnp.where(lane + 512 == idx, 1.0, 0.0).astype(BF)
        weight = dot(pick_own, wown_ref[...]) + dot(pick_oth, woth_ref[...])
        for level in range(LEVELS):
            lw_s[256 * b : 256 * b + 256, level * D : level * D + D] = (
                weight * mix_ref[:, level : level + 1]
            ).astype(BF)
    for level in range(LEVELS):
        tok = dot(a_s[...], lw_s[:, level * D : level * D + D]).astype(BF).astype(F32)
        for w in range(WINDOWS):
            t_s[w * WTOK + level * 72 : w * WTOK + level * 72 + 72, :] = tok[w * 72 : w * 72 + 72]

    def norm_step(w, carry):
        rows = pl.ds(pl.multiple_of(w * WTOK, WTOK), WTOK)
        x = t_s[rows, :]
        centred = x - jnp.mean(x, axis=-1, keepdims=True)
        inv = lax.rsqrt(jnp.mean(centred * centred, axis=-1, keepdims=True) + EPS)
        unit = centred * inv
        unit_s[rows, :] = unit
        inv_s[rows, :] = inv
        norm_s[rows, :] = (unit * gain).astype(BF)
        return carry

    lax.fori_loop(0, WINDOWS, norm_step, 0)
    for n in range(3):
        qkv_s[:, n * D : n * D + D] = dot(norm_s[...], wqkv_ref[:, n * D : n * D + D]).astype(BF)

    gb = dot(tok_ref[:, :PATCHES], cown_ref[...])
    gb = gb + dot(tok_ref[:, PATCHES:TOKENS], cnext_ref[...])
    gb = gb + dot(tok_ref[:, TOKENS:], cedge_ref[...])
    gb_s[...] = gb.astype(BF)
    ga_s[...] = dot(gb_s[...], wproj_ref[...], NT).astype(BF)

    lane = lax.broadcasted_iota(jnp.int32, (1, 128), 1)
    low = lane < HDIM
    keep = [
        jnp.where(low, 1.0, 0.0).astype(BF),
        jnp.where(low, 0.0, 1.0).astype(BF),
    ]

    def window_step(w, carry):
        rows = pl.ds(pl.multiple_of(w * WTOK, WTOK), WTOK)
        same = mcol_ref[w] == mrow_ref[w]
        for pair in range(HEADS // 2):
            at = pair * 128
            q2 = qkv_s[rows, at : at + 128]
            k2 = qkv_s[rows, D + at : D + at + 128]
            v2 = qkv_s[rows, 2 * D + at : 2 * D + at + 128]
            g2 = ga_s[rows, at : at + 128]
            parts = []
            for e in range(2):
                score = dot(q2 * (keep[e] * 0.125), k2, NT)
                score = jnp.where(same, score, -1e30)
                ex = jnp.exp(score - jnp.max(score, axis=-1, keepdims=True))
                prob = ex * (1.0 / jnp.sum(ex, axis=-1, keepdims=True))
                half_prob = prob.astype(BF)
                out = dot(half_prob, v2)
                gv = dot(half_prob, g2, TN)
                gprob = dot(g2 * keep[e], v2, NT)
                centred = gprob - jnp.sum(prob * gprob, axis=-1, keepdims=True)
                gscore = (prob * centred * 0.125).astype(BF)
                gq = dot(gscore, k2)
                gk = dot(gscore, q2, TN)
                parts.append((out, gq, gk, gv))
            out, gq, gk, gv = (jnp.where(low, x, y).astype(BF) for x, y in zip(*parts))
            att_s[rows, at : at + 128] = out
            gp_s[rows, at : at + 128] = gq
            gp_s[rows, D + at : D + at + 128] = gk
            gp_s[rows, 2 * D + at : 2 * D + at + 128] = gv
        return carry

    lax.fori_loop(0, WINDOWS, window_step, 0)

    branch = dot(att_s[...], wproj_ref[...]).astype(BF).astype(F32)
    bo_s[...] = (t_s[...] + branch).astype(BF)
    top_ref[...] = dot(tokt_ref[:PATCHES], bo_s[...]).astype(BF)
    bot_ref[...] = dot(tokt_ref[PATCHES:TOKENS], bo_s[...]).astype(BF)
    edge_ref[...] = dot(tokt_ref[TOKENS:], bo_s[...]).astype(BF)

    for ref, which in ((gown_ref, core), (goth_ref, 1 - core)):
        at = pl.multiple_of(which * 768, 256)
        ref[:, 0:768] = dot(norm_s[...], gp_s[:, pl.ds(at, 768)], TN).astype(BF)
        at = pl.multiple_of(which * 256, 256)
        ref[:, 768:1024] = dot(att_s[...], gb_s[:, pl.ds(at, 256)], TN).astype(BF)

    for w in range(WINDOWS):
        rows = slice(w * WTOK, w * WTOK + WTOK)
        h = dot(gp_s[rows, :], wqkv_ref[...], NT) * gain
        unit = unit_s[rows, :]
        shifted = inv_s[rows, :] * (
            h
            - jnp.mean(h, axis=-1, keepdims=True)
            - unit * jnp.mean(h * unit, axis=-1, keepdims=True)
        )
        total = (gb_s[rows, :].astype(F32) + shifted.astype(BF).astype(F32)).astype(BF).astype(F32)
        for level in range(LEVELS):
            gt_s[level, w * 72 : w * 72 + 72, :] = total[level * 72 : level * 72 + 72]

    for b in range(PSIDE):
        slot = None
        for level in range(LEVELS):
            part = dot(at_s[256 * b : 256 * b + 256, :], gt_s[level].astype(BF))
            part = part * mix_ref[:, level : level + 1]
            slot = part if slot is None else slot + part
        gs_s[256 * b : 256 * b + 256, :] = slot.astype(BF)
    row = lax.broadcasted_iota(jnp.int32, (512, 1024), 0)
    idx = idxr_ref[...]
    for ref, offset in ((gown_ref, 0), (goth_ref, 512)):
        pick = jnp.where(row + offset == idx, 1.0, 0.0).astype(BF)
        ref[:, 1024:1536] = dot(pick, gs_s[...]).astype(BF)


def shape(*dims, dtype=BF):
    return jax.ShapeDtypeStruct(dims, dtype)


def vmem_call(kernel, outs, scratch=(), smem_first=False, count=0):
    specs = [pl.BlockSpec(memory_space=pltpu.VMEM)] * count
    if smem_first:
        specs[0] = pl.BlockSpec(memory_space=pltpu.SMEM)
    many = isinstance(outs, (list, tuple))
    vm = pl.BlockSpec(memory_space=pltpu.VMEM)
    return pl.pallas_call(
        kernel,
        out_shape=outs,
        in_specs=specs,
        out_specs=[vm] * len(outs) if many else vm,
        scratch_shapes=list(scratch),
        compiler_params=pltpu.CompilerParams(vmem_limit_bytes=VMEM_LIMIT),
    )


def per_device(
    counts,
    pixels,
    var_order,
    embed_weight,
    level_mix,
    norm_gain,
    w_qkv,
    w_proj,
    mask_ids,
    cotangent,
):
    chips, lats, lons = counts
    bands = chips * 2
    lat = lax.axis_index("lat")
    core = lax.axis_index("core")
    lon = lax.axis_index("lon")
    info = jnp.stack([lat, core]).astype(jnp.int32)
    rows_ring = ("chip", "core", "lat")
    everyone = ("chip", "core", "lat", "lon")
    ring = bands * lats
    group = ("chip", "lat", "lon")
    group_size = chips * lats * lons

    swap_lon = [(0, 1), (1, 0)]
    swap_core = [(0, 1), (1, 0)]

    own_weight = lax.all_gather(embed_weight.reshape(32, D), "chip", axis=0, tiled=True)
    oth_weight = lax.ppermute(own_weight, "core", swap_core)

    cot_first = cotangent[:HALF]
    cot_next = lax.ppermute(cot_first, rows_ring, [(i, (i - 1) % ring) for i in range(ring)])
    strip_first = cotangent[:HALF, :, :3].reshape(36, D)
    strip_last = cotangent[HALF:, :, :3].reshape(36, D)
    east = lax.ppermute(strip_last, "lon", swap_lon)
    north_east = lax.ppermute(
        strip_first,
        everyone,
        [(i * 2 + k, ((i - 1) % ring) * 2 + 1 - k) for i in range(ring) for k in range(2)],
    )
    cot_edge = jnp.concatenate([east, north_east, jnp.zeros((128 - 72, D), BF)], axis=0)

    place_e = jnp.asarray(edge_place(), BF)
    main, edge = pixel_place()
    border = vmem_call(edge_kernel, shape(2, bands * 8, 128), count=2)(pixels, place_e)
    halo = lax.ppermute(border, "lon", swap_lon)
    packed = vmem_call(pack_kernel, shape(bands, 2, 8, LANES), smem_first=True, count=5)(
        info, pixels, jnp.asarray(main, BF), jnp.asarray(edge, BF), halo
    )
    recv = lax.all_to_all(
        packed.reshape(bands * 2, 8, LANES), rows_ring, split_axis=0, concat_axis=0, tiled=True
    ).reshape(bands, 2, 8, LANES)

    device = var_order // 2
    base = jnp.where(device % 2 == core, 0, 512) + (device // 2) * 32 + (var_order % 2) * 16
    index = base[None, :, None] + (
        jnp.arange(4)[:, None, None] + 4 * jnp.arange(4)[None, None, :]
    )
    index = index.reshape(1024).astype(jnp.int32)
    slot_mix = jnp.repeat(level_mix[var_order], 4, axis=0)

    ids = mask_ids.reshape(2, HALF, LEVELS, WINDOWS, WCOL).transpose(3, 2, 0, 1, 4)
    ids = ids.reshape(WINDOWS, WTOK)

    pmain, prest = patch_place()
    tok = token_place()
    top, bot, strip, gown, goth = vmem_call(
        block_kernel,
        [
            shape(PATCHES, D),
            shape(PATCHES, D),
            shape(128, D),
            shape(512, 1536),
            shape(512, 1536),
        ],
        [
            pltpu.VMEM((PATCHES, 1024), BF),
            pltpu.VMEM((1024, PATCHES), BF),
            pltpu.VMEM((1024, 1024), BF),
            pltpu.VMEM((TOKENS, D), F32),
            pltpu.VMEM((TOKENS, D), F32),
            pltpu.VMEM((TOKENS, 1), F32),
            pltpu.VMEM((TOKENS, D), BF),
            pltpu.VMEM((TOKENS, 3 * D), BF),
            pltpu.VMEM((TOKENS, D), BF),
            pltpu.VMEM((TOKENS, D), BF),
            pltpu.VMEM((TOKENS, D), BF),
            pltpu.VMEM((TOKENS, 3 * D), BF),
            pltpu.VMEM((TOKENS, D), BF),
            pltpu.VMEM((LEVELS, PATCHES, D), F32),
            pltpu.VMEM((1024, D), BF),
        ],
        smem_first=True,
        count=19,
    )(
        info,
        recv,
        own_weight,
        oth_weight,
        index[:, None],
        index[None, :],
        slot_mix,
        norm_gain[None, :],
        w_qkv,
        w_proj,
        ids[:, :, None],
        ids[:, None, :],
        cotangent[HALF:].reshape(PATCHES, D),
        cot_next.reshape(PATCHES, D),
        cot_edge,
        jnp.asarray(pmain, BF),
        jnp.asarray(prest, BF),
        jnp.asarray(tok, BF),
        jnp.asarray(tok.T, BF),
    )

    from_core = lax.ppermute(goth, "core", swap_core)
    chip_sum = (gown.astype(F32) + from_core.astype(F32)).astype(BF)
    terms = lax.all_to_all(
        chip_sum.reshape(group_size, 8, 1536), group, split_axis=0, concat_axis=0, tiled=True
    )
    owned = jnp.sum(terms.astype(F32), axis=0).astype(BF)
    copies = jnp.broadcast_to(owned[None, :, :1024], (group_size, 8, 1024))
    mine = lax.all_to_all(copies, group, split_axis=0, concat_axis=0, tiled=True)
    mine = mine.reshape(512, 1024)
    other = lax.ppermute(mine, "core", swap_core)
    first = jnp.where(core == 0, mine, other).astype(F32)
    second = jnp.where(core == 0, other, mine).astype(F32)
    grad_qkv = jnp.concatenate([first[:, :768], second[:, :768]], axis=1)
    grad_proj = jnp.concatenate([first[:, 768:], second[:, 768:]], axis=1)

    embed_part = owned[:, 1024:]
    pieces = [embed_part]
    for dlat, dlon in ((0, 1), (1, 0), (1, 1)):
        pieces.append(
            lax.ppermute(
                embed_part,
                ("lat", "lon"),
                [(i * 2 + k, (i ^ dlat) * 2 + (k ^ dlon)) for i in range(2) for k in range(2)],
            )
        )
    stacked = jnp.stack(pieces)
    tile = lat * 2 + lon
    grad_embed = jnp.concatenate(
        [lax.dynamic_index_in_dim(stacked, tile ^ t, 0, keepdims=False) for t in range(4)], axis=0
    )
    grad_embed = grad_embed.reshape(2, 16, D).astype(F32)

    from_before = lax.ppermute(bot, rows_ring, [(i, (i + 1) % ring) for i in range(ring)])
    west = lax.ppermute(strip[:36], "lon", swap_lon)
    south_west = lax.ppermute(
        strip[36:72],
        everyone,
        [(i * 2 + k, ((i + 1) % ring) * 2 + 1 - k) for i in range(ring) for k in range(2)],
    )
    body = jnp.concatenate([from_before, top], axis=0).reshape(ROWS, LEVELS, COLS, D)
    sides = jnp.concatenate([south_west, west], axis=0).reshape(ROWS, LEVELS, 3, D)
    block_out = jnp.concatenate([sides, body[:, :, 3:]], axis=2)
    return (block_out, grad_embed, grad_qkv, grad_proj)


def solution(mesh):
    var, lats, lons = (mesh.shape[name] for name in ("var", "lat", "lon"))
    chips = var // 2
    fine = Mesh(mesh.devices.reshape(chips, 2, lats, lons), ("chip", "core", "lat", "lon"))
    both = ("chip", "core")
    in_specs = (
        P(None, "lat", both, None, "lon"),
        P(),
        P(both, None, None),
        P(),
        P(),
        P(),
        P(),
        P(("chip", "core", "lat"), None, "lon"),
        P(("chip", "core", "lat"), None, "lon", None),
    )
    out_specs = (P(("chip", "core", "lat"), None, "lon", None), P(both, None, None), P(), P())
    return jax.shard_map(
        functools.partial(per_device, (chips, lats, lons)),
        mesh=fine,
        in_specs=in_specs,
        out_specs=out_specs,
        check_vma=False,
    )
```

```python
import functools

import jax
import jax.numpy as jnp
import numpy as np
from jax import lax
from jax.experimental import pallas as pl
from jax.experimental.pallas import tpu as pltpu
from jax.sharding import Mesh, PartitionSpec as P

D = 512
HEADS = 8
HDIM = 64
PSIDE = 4
WCOL = 6
ROWS = 12
HALF = 6
COLS = 48
WINDOWS = 8
LEVELS = 2
TOKENS = 1152
WTOK = 144
PATCHES = 576
LANES = 1152
STRIP = 48
EPS = 1e-05
BF = jnp.bfloat16
F32 = jnp.float32

NN = (((1,), (0,)), ((), ()))
NT = (((1,), (1,)), ((), ()))
TN = (((0,), (0,)), ((), ()))


def dot(a, b, dims=NN):
    return lax.dot_general(a, b, dims, preferred_element_type=F32)


def patch_index(w, j, c6):
    if w == WINDOWS - 1:
        return 252 + j * 3 + c6 if c6 < 3 else 267 + j * 3 + c6
    return w * 36 + j * WCOL + c6


def pixel_lane(b, patch):
    return 256 * b + patch if patch < 256 else 1024 + 32 * b + patch - 256


def edge_place():
    place = np.zeros((HALF, 128, 128), np.float32)
    for j in range(HALF):
        lane = np.arange(12)
        place[j, lane, j * 12 + lane] = 1
    return place


def pixel_place():
    main = np.zeros((HALF * PSIDE * COLS, LANES), np.float32)
    edge = np.zeros((128, 128), np.float32)
    for j in range(HALF):
        for c in range(COLS):
            for b in range(PSIDE):
                col = c - 3 if c >= 3 else COLS - 3 + c
                lane = pixel_lane(b, patch_index(col // WCOL, j, col % WCOL))
                if c >= 3:
                    main[(j * COLS + c) * PSIDE + b, lane] = 1
                else:
                    edge[j * 12 + c * PSIDE + b, lane - 1024] = 1
    return main, edge


def patch_place():
    main = np.zeros((2, PATCHES, 256), np.float32)
    rest = np.zeros((2, PSIDE, PATCHES, 128), np.float32)
    for half in range(2):
        for w in range(WINDOWS):
            for i in range(36):
                patch = patch_index(w, i // WCOL, i % WCOL)
                row = w * 72 + half * 36 + i
                if patch < 256:
                    main[half, row, patch] = 1
                else:
                    for b in range(PSIDE):
                        rest[half, b, row, 32 * b + patch - 256] = 1
    return main, rest


def token_place():
    place = np.zeros((TOKENS, TOKENS + 128), np.float32)
    for w in range(WINDOWS):
        for level in range(LEVELS):
            for half in range(2):
                for j in range(HALF):
                    for c6 in range(WCOL):
                        t = w * WTOK + level * 72 + half * 36 + j * WCOL + c6
                        c = w * WCOL + c6 + 3
                        if c < COLS:
                            place[t, half * PATCHES + (j * LEVELS + level) * COLS + c] = 1
                        else:
                            place[t, TOKENS + half * STRIP + (j * LEVELS + level) * 3 + c - COLS] = 1
    return place


def half_rows(pix_ref, half, j, lanes):
    rows = pix_ref[:, half * HALF + j, :, :, :lanes].astype(F32)
    merged = jnp.concatenate([rows[:, 0], rows[:, 1]], axis=1)
    return merged.reshape(merged.shape[0] * 8, lanes)


def strip_place():
    place = np.zeros((2 * STRIP, ROWS * LEVELS * 16), np.float32)
    for half in range(2):
        for i in range(HALF * LEVELS):
            for c in range(3):
                place[half * STRIP + i * 3 + c, (half * HALF * LEVELS + i) * 16 + c] = 1
    return place


def edge_kernel(
    pix_ref, cot_ref, weight_ref, place_ref, strip_ref, west_ref, ahead_ref, corner_ref, copies_ref
):
    size = (west_ref.shape[0] - 4 * STRIP) // 2
    for half in range(2):
        total = None
        for j in range(HALF):
            term = dot(half_rows(pix_ref, half, j, 128).astype(BF), place_ref[j])
            total = term if total is None else total + term
        west_ref[half * size : half * size + size, :] = total.astype(BF)
    strips = cot_ref[:, :, :16, :].reshape(ROWS * LEVELS * 16, D)
    strips = dot(strip_ref[...], strips).astype(BF)
    corner_ref[...] = strips[:STRIP]
    for t in range(4):
        at = 2 * size + t * STRIP
        west_ref[at : at + STRIP, :] = strips[STRIP:, 128 * t : 128 * t + 128]
    ahead_ref[...] = cot_ref[:HALF].reshape(PATCHES, D)
    copies_ref[...] = jnp.broadcast_to(weight_ref[...][None], copies_ref.shape)


def store_half(out_ref, half, lat, lanes, block):
    bands = out_ref.shape[0]
    if half == 1:
        out_ref[:, lat, :, lanes] = block
        return

    @pl.when(lat == 0)
    def _():
        out_ref[: bands - 1, 1, :, lanes] = block[1:]
        out_ref[bands - 1 :, 1, :, lanes] = block[:1]

    @pl.when(lat == 1)
    def _():
        out_ref[:, 0, :, lanes] = block


def pack_kernel(info_ref, pix_ref, main_ref, out_ref, rows_s):
    bands = out_ref.shape[0]
    size = bands * 8
    for half in range(2):
        for i in range(HALF // 2):
            pair = [half_rows(pix_ref, half, 2 * i + k, 4 * COLS) for k in range(2)]
            rows_s[half * size : half * size + size, 384 * i : 384 * i + 384] = jnp.concatenate(
                pair, axis=1
            ).astype(BF)
    for n in range(3):
        lanes = slice(384 * n, 384 * n + 384)
        block = dot(rows_s[...], main_ref[:, lanes])
        for half in range(2):
            part = block[half * size : half * size + size].reshape(bands, 8, 384).astype(BF)
            store_half(out_ref, half, info_ref[0], lanes, part)


def halo_kernel(info_ref, packed_ref, edge_ref, halo_ref, out_ref):
    bands = out_ref.shape[0]
    lat = info_ref[0]
    for half in range(2):
        rows = halo_ref[half * bands * 8 : (half + 1) * bands * 8, :]
        block = dot(rows, edge_ref[...]).reshape(bands, 8, 128)
        store_half(out_ref, half, lat, slice(0, 128), block.astype(BF))
    out_ref[...] = out_ref[...] + packed_ref[...]


def prepare_kernel(
    idx_ref,
    mix_ref,
    wown_ref,
    woth_ref,
    cot_ref,
    ahead_ref,
    halo_ref,
    corner_ref,
    tok_ref,
    wproj_ref,
    lw_ref,
    gb_ref,
    ga_ref,
):
    start = halo_ref.shape[0] - 4 * STRIP
    east = jnp.concatenate(
        [halo_ref[start + STRIP * t : start + STRIP * t + STRIP, :] for t in range(4)], axis=1
    )
    sides = jnp.concatenate([east, corner_ref[...], jnp.zeros((128 - 2 * STRIP, D), BF)], axis=0)
    gb = dot(tok_ref[:, :PATCHES], cot_ref[HALF:].reshape(PATCHES, D))
    gb = gb + dot(tok_ref[:, PATCHES:TOKENS], ahead_ref[...])
    gb = gb + dot(tok_ref[:, TOKENS:], sides)
    gb_ref[...] = gb.astype(BF)
    ga_ref[...] = dot(gb_ref[...], wproj_ref[...], NT).astype(BF)
    lane = lax.broadcasted_iota(jnp.int32, (256, 512), 1)
    for b in range(PSIDE):
        at = slice(256 * b, 256 * b + 256)
        idx = idx_ref[at, :]
        weight = dot(jnp.where(lane == idx, 1.0, 0.0).astype(BF), wown_ref[...])
        weight = weight + dot(jnp.where(lane + 512 == idx, 1.0, 0.0).astype(BF), woth_ref[...])
        for level in range(LEVELS):
            lw_ref[at, level * D : level * D + D] = (
                weight * mix_ref[:, level : level + 1]
            ).astype(BF)


def block_kernel(
    info_ref,
    recv_ref,
    lw_ref,
    gb_ref,
    ga_ref,
    idxr_ref,
    mix_ref,
    gain_ref,
    wqkv_ref,
    wproj_ref,
    mcol_ref,
    mrow_ref,
    pmain_ref,
    prest_ref,
    tokt_ref,
    top_ref,
    bot_ref,
    side_top_ref,
    side_bot_ref,
    gown_ref,
    goth_ref,
    a_s,
    at_s,
    t_s,
    unit_s,
    inv_s,
    norm_s,
    qkv_s,
    att_s,
    gp_s,
    bo_s,
    gt_s,
    gs_s,
):
    lat = info_ref[0]
    core = info_ref[1]
    gain = gain_ref[...]

    halves = []
    for half in range(2):
        src = lat if half == 0 else 1 - lat
        part = recv_ref[:, src].astype(F32)
        halves.append(part.reshape(256, LANES).astype(BF))
    for b in range(PSIDE):
        rows = None
        columns = None
        for half in range(2):
            main = halves[half][:, 256 * b : 256 * b + 256]
            rest = halves[half][:, 1024:1152]
            r = dot(pmain_ref[half], main, NT) + dot(prest_ref[half, b], rest, NT)
            c = dot(main, pmain_ref[half], NT) + dot(rest, prest_ref[half, b], NT)
            rows = r if rows is None else rows + r
            columns = c if columns is None else columns + c
        a_s[:, 256 * b : 256 * b + 256] = rows.astype(BF)
        at_s[256 * b : 256 * b + 256, :] = columns.astype(BF)
    for level in range(LEVELS):
        tok = dot(a_s[...], lw_ref[:, level * D : level * D + D]).astype(BF).astype(F32)
        for w in range(WINDOWS):
            t_s[w * WTOK + level * 72 : w * WTOK + level * 72 + 72, :] = tok[w * 72 : w * 72 + 72]

    def norm_step(w, carry):
        rows = pl.ds(pl.multiple_of(w * WTOK, WTOK), WTOK)
        x = t_s[rows, :]
        centred = x - jnp.mean(x, axis=-1, keepdims=True)
        inv = lax.rsqrt(jnp.mean(centred * centred, axis=-1, keepdims=True) + EPS)
        unit = centred * inv
        unit_s[rows, :] = unit
        inv_s[rows, :] = inv
        norm_s[rows, :] = (unit * gain).astype(BF)
        return carry

    lax.fori_loop(0, WINDOWS, norm_step, 0)
    for n in range(3):
        qkv_s[:, n * D : n * D + D] = dot(norm_s[...], wqkv_ref[:, n * D : n * D + D]).astype(BF)

    low = lax.broadcasted_iota(jnp.int32, (1, 128), 1) < HDIM
    lane = lax.broadcasted_iota(jnp.int32, (1, 256), 1) // HDIM
    keep = [jnp.where(lane == e, 1.0, 0.0).astype(BF) for e in range(4)]

    def by_head(x):
        return jnp.concatenate([x * keep[e] for e in range(4)], axis=0)

    def own_heads(x):
        left = jnp.where(low, x[:WTOK, :128], x[WTOK : 2 * WTOK, :128])
        right = jnp.where(low, x[2 * WTOK : 3 * WTOK, 128:], x[3 * WTOK :, 128:])
        return jnp.concatenate([left, right], axis=1).astype(BF)

    def window_step(w, carry):
        rows = pl.ds(pl.multiple_of(w * WTOK, WTOK), WTOK)
        same = mcol_ref[w] == mrow_ref[w]
        for part in range(2):
            at = part * 256
            keys = qkv_s[rows, D + at : D + at + 256]
            values = qkv_s[rows, 2 * D + at : 2 * D + at + 256]
            queries = by_head(qkv_s[rows, at : at + 256] * 0.125)
            grads = by_head(ga_ref[rows, at : at + 256])
            score = jnp.where(same, dot(keys, queries, NT), -1e30)
            ex = jnp.exp(score - jnp.max(score, axis=0, keepdims=True))
            prob = ex * (1.0 / jnp.sum(ex, axis=0, keepdims=True))
            gprob = dot(values, grads, NT)
            centred = gprob - jnp.sum(prob * gprob, axis=0, keepdims=True)
            gscore = (prob * centred).astype(BF)
            prob = prob.astype(BF)
            att_s[rows, at : at + 256] = own_heads(dot(prob, values, TN))
            gp_s[rows, at : at + 256] = own_heads(dot(gscore, keys * 0.125, TN))
            gp_s[rows, D + at : D + at + 256] = dot(gscore, queries).astype(BF)
            gp_s[rows, 2 * D + at : 2 * D + at + 256] = dot(prob, grads).astype(BF)
        return carry

    lax.fori_loop(0, WINDOWS, window_step, 0)

    branch = dot(att_s[...], wproj_ref[...]).astype(BF).astype(F32)
    bo_s[...] = (t_s[...] + branch).astype(BF)
    top_ref[...] = dot(tokt_ref[:PATCHES], bo_s[...]).astype(BF)
    bot_ref[...] = dot(tokt_ref[PATCHES:TOKENS], bo_s[...]).astype(BF)
    sides = dot(tokt_ref[TOKENS:], bo_s[...]).astype(BF)
    side_top_ref[...] = sides[:STRIP]
    side_bot_ref[...] = sides[STRIP : 2 * STRIP]

    for ref, which in ((gown_ref, core), (goth_ref, 1 - core)):
        at = pl.multiple_of(which * 768, 256)
        ref[:, 0:768] = dot(norm_s[...], gp_s[:, pl.ds(at, 768)], TN).astype(BF)
        at = pl.multiple_of(which * 256, 256)
        ref[:, 768:1024] = dot(att_s[...], gb_ref[:, pl.ds(at, 256)], TN).astype(BF)

    for w in range(WINDOWS):
        rows = slice(w * WTOK, w * WTOK + WTOK)
        h = dot(gp_s[rows, :], wqkv_ref[...], NT) * gain
        unit = unit_s[rows, :]
        shifted = inv_s[rows, :] * (
            h
            - jnp.mean(h, axis=-1, keepdims=True)
            - unit * jnp.mean(h * unit, axis=-1, keepdims=True)
        )
        total = (gb_ref[rows, :].astype(F32) + shifted.astype(BF).astype(F32)).astype(BF).astype(F32)
        for level in range(LEVELS):
            gt_s[level, w * 72 : w * 72 + 72, :] = total[level * 72 : level * 72 + 72]

    for b in range(PSIDE):
        slot = None
        for level in range(LEVELS):
            part = dot(at_s[256 * b : 256 * b + 256, :], gt_s[level].astype(BF))
            part = part * mix_ref[:, level : level + 1]
            slot = part if slot is None else slot + part
        gs_s[256 * b : 256 * b + 256, :] = slot.astype(BF)
    row = lax.broadcasted_iota(jnp.int32, (512, 1024), 0)
    idx = idxr_ref[...]
    for ref, offset in ((gown_ref, 0), (goth_ref, 512)):
        pick = jnp.where(row + offset == idx, 1.0, 0.0).astype(BF)
        ref[:, 1024:1536] = dot(pick, gs_s[...]).astype(BF)


def shape(*dims, dtype=BF):
    return jax.ShapeDtypeStruct(dims, dtype)


def cost(us):
    return pl.CostEstimate(flops=int(us * 1e9), bytes_accessed=0, transcendentals=0)


def vmem_call(kernel, outs, scratch=(), smem_first=False, count=0, mib=58, us=1):
    specs = [pl.BlockSpec(memory_space=pltpu.VMEM)] * count
    if smem_first:
        specs[0] = pl.BlockSpec(memory_space=pltpu.SMEM)
    many = isinstance(outs, (list, tuple))
    vm = pl.BlockSpec(memory_space=pltpu.VMEM)
    return pl.pallas_call(
        kernel,
        out_shape=outs,
        in_specs=specs,
        out_specs=[vm] * len(outs) if many else vm,
        scratch_shapes=list(scratch),
        compiler_params=pltpu.CompilerParams(vmem_limit_bytes=mib * 1024 * 1024),
        cost_estimate=cost(us),
    )


def per_device(
    counts,
    pixels,
    var_order,
    embed_weight,
    level_mix,
    norm_gain,
    w_qkv,
    w_proj,
    mask_ids,
    cotangent,
):
    chips, lats, lons = counts
    bands = chips * 2
    lat = lax.axis_index("lat")
    core = lax.axis_index("core")
    lon = lax.axis_index("lon")
    info = jnp.stack([lat, core]).astype(jnp.int32)
    rows_ring = ("chip", "core", "lat")
    everyone = ("chip", "core", "lat", "lon")
    ring = bands * lats
    group = ("chip", "lat", "lon")
    group_size = chips * lats * lons

    swap_lon = [(0, 1), (1, 0)]
    swap_core = [(0, 1), (1, 0)]

    main, edge = pixel_place()
    border, ahead, corner, copies = vmem_call(
        edge_kernel,
        [
            shape(2 * bands * 8 + 4 * STRIP, 128),
            shape(PATCHES, D),
            shape(STRIP, D),
            shape(chips, 32, D),
        ],
        count=5,
        us=3,
    )(
        pixels,
        cotangent,
        embed_weight.reshape(32, D),
        jnp.asarray(edge_place(), BF),
        jnp.asarray(strip_place(), BF),
    )
    halo = lax.ppermute(border, "lon", swap_lon)
    ahead = lax.ppermute(ahead, rows_ring, [(i, (i - 1) % ring) for i in range(ring)])
    corner = lax.ppermute(
        corner,
        everyone,
        [(i * 2 + k, ((i - 1) % ring) * 2 + 1 - k) for i in range(ring) for k in range(2)],
    )
    own_weight = lax.all_to_all(copies, "chip", split_axis=0, concat_axis=0, tiled=True)
    own_weight = own_weight.reshape(512, D)
    oth_weight = lax.ppermute(own_weight, "core", swap_core)

    packed = vmem_call(
        pack_kernel,
        shape(bands, 2, 8, LANES),
        [pltpu.VMEM((2 * bands * 8, LANES), BF)],
        smem_first=True,
        count=3,
        us=6,
    )(info, pixels, jnp.asarray(main, BF))
    halo, ahead, corner = lax.optimization_barrier((halo, ahead, corner))
    vm = pl.BlockSpec(memory_space=pltpu.VMEM)
    last = pl.BlockSpec((bands, 2, 8, 128), lambda i: (0, 0, 0, LANES // 128 - 1))
    packed = pl.pallas_call(
        halo_kernel,
        grid=(1,),
        out_shape=shape(bands, 2, 8, LANES),
        in_specs=[pl.BlockSpec(memory_space=pltpu.SMEM), last, vm, vm],
        out_specs=last,
        input_output_aliases={1: 0},
        compiler_params=pltpu.CompilerParams(vmem_limit_bytes=58 * 1024 * 1024),
        cost_estimate=cost(2),
    )(info, packed, jnp.asarray(edge, BF), halo)
    recv = lax.all_to_all(
        packed.reshape(bands * 2, 8, LANES), rows_ring, split_axis=0, concat_axis=0, tiled=True
    ).reshape(bands, 2, 8, LANES)

    device = var_order // 2
    base = jnp.where(device % 2 == core, 0, 512) + (device // 2) * 32 + (var_order % 2) * 16
    index = base[None, :, None] + (
        jnp.arange(4)[:, None, None] + 4 * jnp.arange(4)[None, None, :]
    )
    index = index.reshape(1024).astype(jnp.int32)
    slot_mix = jnp.repeat(level_mix[var_order], 4, axis=0)

    ids = mask_ids.reshape(2, HALF, LEVELS, WINDOWS, WCOL).transpose(3, 2, 0, 1, 4)
    ids = ids.reshape(WINDOWS, WTOK)

    tok = token_place()
    level_weight, grad_branch, grad_attended = vmem_call(
        prepare_kernel, [shape(1024, 1024), shape(TOKENS, D), shape(TOKENS, D)], count=10, us=8
    )(
        index[:, None],
        slot_mix,
        own_weight,
        oth_weight,
        cotangent,
        ahead,
        halo,
        corner,
        jnp.asarray(tok, BF),
        w_proj,
    )

    pmain, prest = patch_place()
    top, bot, side_top, side_bot, gown, goth = vmem_call(
        block_kernel,
        [
            shape(PATCHES, D),
            shape(PATCHES, D),
            shape(STRIP, D),
            shape(STRIP, D),
            shape(512, 1536),
            shape(512, 1536),
        ],
        [
            pltpu.VMEM((PATCHES, 1024), BF),
            pltpu.VMEM((1024, PATCHES), BF),
            pltpu.VMEM((TOKENS, D), F32),
            pltpu.VMEM((TOKENS, D), F32),
            pltpu.VMEM((TOKENS, 1), F32),
            pltpu.VMEM((TOKENS, D), BF),
            pltpu.VMEM((TOKENS, 3 * D), BF),
            pltpu.VMEM((TOKENS, D), BF),
            pltpu.VMEM((TOKENS, 3 * D), BF),
            pltpu.VMEM((TOKENS, D), BF),
            pltpu.VMEM((LEVELS, PATCHES, D), F32),
            pltpu.VMEM((1024, D), BF),
        ],
        smem_first=True,
        count=15,
        us=38,
    )(
        info,
        recv,
        level_weight,
        grad_branch,
        grad_attended,
        index[None, :],
        slot_mix,
        norm_gain[None, :],
        w_qkv,
        w_proj,
        ids[:, :, None],
        jnp.tile(ids, (1, 4))[:, None, :],
        jnp.asarray(pmain, BF),
        jnp.asarray(prest, BF),
        jnp.asarray(tok.T, BF),
    )

    from_core = lax.ppermute(goth, "core", swap_core)
    chip_sum = (gown.astype(F32) + from_core.astype(F32)).astype(BF)
    terms = lax.all_to_all(
        chip_sum.reshape(group_size, 8, 1536), group, split_axis=0, concat_axis=0, tiled=True
    )
    owned = jnp.sum(terms.astype(F32), axis=0).astype(BF)
    copies = jnp.broadcast_to(owned[None, :, :1024], (group_size, 8, 1024))
    mine = lax.all_to_all(copies, group, split_axis=0, concat_axis=0, tiled=True)
    mine = mine.reshape(512, 1024)

    embed_part = owned[:, 1024:]
    pieces = [embed_part]
    for dlat, dlon in ((0, 1), (1, 0), (1, 1)):
        pieces.append(
            lax.ppermute(
                embed_part,
                ("lat", "lon"),
                [(i * 2 + k, (i ^ dlat) * 2 + (k ^ dlon)) for i in range(2) for k in range(2)],
            )
        )
    stacked = jnp.stack(pieces)
    tile = lat * 2 + lon
    grad_embed = jnp.concatenate(
        [lax.dynamic_index_in_dim(stacked, tile ^ t, 0, keepdims=False) for t in range(4)], axis=0
    )
    grad_embed = grad_embed.reshape(2, 16, D).astype(F32)

    from_before = lax.ppermute(bot, rows_ring, [(i, (i + 1) % ring) for i in range(ring)])
    west = lax.ppermute(side_top, "lon", swap_lon)
    south_west = lax.ppermute(
        side_bot,
        everyone,
        [(i * 2 + k, ((i + 1) % ring) * 2 + 1 - k) for i in range(ring) for k in range(2)],
    )
    _, from_before, west, south_west = lax.optimization_barrier((owned, from_before, west, south_west))
    body = jnp.concatenate([from_before, top], axis=0).reshape(ROWS, LEVELS, COLS, D)
    sides = jnp.concatenate([south_west[:36], west[:36]], axis=0).reshape(ROWS, LEVELS, 3, D)
    block_out = jnp.concatenate([sides, body[:, :, 3:]], axis=2)

    mine, block_out, grad_embed = lax.optimization_barrier((mine, block_out, grad_embed))
    other = lax.ppermute(mine, "core", swap_core)
    first = jnp.where(core == 0, mine, other).astype(F32)
    second = jnp.where(core == 0, other, mine).astype(F32)
    grad_qkv = jnp.concatenate([first[:, :768], second[:, :768]], axis=1)
    grad_proj = jnp.concatenate([first[:, 768:], second[:, 768:]], axis=1)
    return (block_out, grad_embed, grad_qkv, grad_proj)


def solution(mesh):
    var, lats, lons = (mesh.shape[name] for name in ("var", "lat", "lon"))
    chips = var // 2
    fine = Mesh(mesh.devices.reshape(chips, 2, lats, lons), ("chip", "core", "lat", "lon"))
    both = ("chip", "core")
    in_specs = (
        P(None, "lat", both, None, "lon"),
        P(),
        P(both, None, None),
        P(),
        P(),
        P(),
        P(),
        P(("chip", "core", "lat"), None, "lon"),
        P(("chip", "core", "lat"), None, "lon", None),
    )
    out_specs = (P(("chip", "core", "lat"), None, "lon", None), P(both, None, None), P(), P())
    return jax.shard_map(
        functools.partial(per_device, (chips, lats, lons)),
        mesh=fine,
        in_specs=in_specs,
        out_specs=out_specs,
        check_vma=False,
    )
```

```python
import functools

import jax
import jax.numpy as jnp
import numpy as np
from jax import lax
from jax.experimental import pallas as pl
from jax.experimental.pallas import tpu as pltpu
from jax.sharding import Mesh, PartitionSpec as P

D = 512
HEADS = 8
HDIM = 64
PSIDE = 4
WCOL = 6
ROWS = 12
HALF = 6
COLS = 48
WINDOWS = 8
LEVELS = 2
TOKENS = 1152
WTOK = 144
PATCHES = 576
LANES = 1152
STRIP = 48
EPS = 1e-05
BF = jnp.bfloat16
F32 = jnp.float32

NN = (((1,), (0,)), ((), ()))
NT = (((1,), (1,)), ((), ()))
TN = (((0,), (0,)), ((), ()))


def dot(a, b, dims=NN):
    return lax.dot_general(a, b, dims, preferred_element_type=F32)


def patch_index(w, j, c6):
    if w == WINDOWS - 1:
        return 252 + j * 3 + c6 if c6 < 3 else 267 + j * 3 + c6
    return w * 36 + j * WCOL + c6


def pixel_lane(b, patch):
    return 256 * b + patch if patch < 256 else 1024 + 32 * b + patch - 256


def edge_place():
    place = np.zeros((HALF, 128, 128), np.float32)
    for j in range(HALF):
        lane = np.arange(12)
        place[j, lane, j * 12 + lane] = 1
    return place


def pixel_place():
    main = np.zeros((HALF * PSIDE * COLS, LANES), np.float32)
    edge = np.zeros((128, 128), np.float32)
    for j in range(HALF):
        for c in range(COLS):
            for b in range(PSIDE):
                col = c - 3 if c >= 3 else COLS - 3 + c
                lane = pixel_lane(b, patch_index(col // WCOL, j, col % WCOL))
                if c >= 3:
                    main[(j * COLS + c) * PSIDE + b, lane] = 1
                else:
                    edge[j * 12 + c * PSIDE + b, lane - 1024] = 1
    return main, edge


def patch_place():
    main = np.zeros((2, PATCHES, 256), np.float32)
    rest = np.zeros((2, PSIDE, PATCHES, 128), np.float32)
    for half in range(2):
        for w in range(WINDOWS):
            for i in range(36):
                patch = patch_index(w, i // WCOL, i % WCOL)
                row = w * 72 + half * 36 + i
                if patch < 256:
                    main[half, row, patch] = 1
                else:
                    for b in range(PSIDE):
                        rest[half, b, row, 32 * b + patch - 256] = 1
    return main, rest


def token_place():
    place = np.zeros((TOKENS, TOKENS + 128), np.float32)
    for w in range(WINDOWS):
        for level in range(LEVELS):
            for half in range(2):
                for j in range(HALF):
                    for c6 in range(WCOL):
                        t = w * WTOK + level * 72 + half * 36 + j * WCOL + c6
                        c = w * WCOL + c6 + 3
                        if c < COLS:
                            place[t, half * PATCHES + (j * LEVELS + level) * COLS + c] = 1
                        else:
                            place[t, TOKENS + half * STRIP + (j * LEVELS + level) * 3 + c - COLS] = 1
    return place


def half_rows(pix_ref, half, j, lanes):
    rows = pix_ref[:, half * HALF + j, :, :, :lanes].astype(F32)
    merged = jnp.concatenate([rows[:, 0], rows[:, 1]], axis=1)
    return merged.reshape(merged.shape[0] * 8, lanes)


def strip_place():
    place = np.zeros((2 * STRIP, ROWS * LEVELS * 16), np.float32)
    for half in range(2):
        for i in range(HALF * LEVELS):
            for c in range(3):
                place[half * STRIP + i * 3 + c, (half * HALF * LEVELS + i) * 16 + c] = 1
    return place


def edge_kernel(
    pix_ref, cot_ref, weight_ref, place_ref, strip_ref, west_ref, ahead_ref, corner_ref, copies_ref
):
    size = (west_ref.shape[0] - 4 * STRIP) // 2
    for half in range(2):
        total = None
        for j in range(HALF):
            term = dot(half_rows(pix_ref, half, j, 128).astype(BF), place_ref[j])
            total = term if total is None else total + term
        west_ref[half * size : half * size + size, :] = total.astype(BF)
    strips = cot_ref[:, :, :16, :].reshape(ROWS * LEVELS * 16, D)
    strips = dot(strip_ref[...], strips).astype(BF)
    corner_ref[...] = strips[:STRIP]
    for t in range(4):
        at = 2 * size + t * STRIP
        west_ref[at : at + STRIP, :] = strips[STRIP:, 128 * t : 128 * t + 128]
    ahead_ref[...] = cot_ref[:HALF]
    copies_ref[...] = jnp.broadcast_to(weight_ref[...][None], copies_ref.shape)


def store_half(out_ref, half, lat, lanes, block):
    bands = out_ref.shape[0]
    if half == 1:
        out_ref[:, lat, :, lanes] = block
        return

    @pl.when(lat == 0)
    def _():
        out_ref[: bands - 1, 1, :, lanes] = block[1:]
        out_ref[bands - 1 :, 1, :, lanes] = block[:1]

    @pl.when(lat == 1)
    def _():
        out_ref[:, 0, :, lanes] = block


def pack_kernel(pix_ref, edge_ref, halo_ref, main_ref, out_ref, rows_s, main_s, sem):
    move = pltpu.make_async_copy(main_ref, main_s, sem)
    move.start()
    lat = lax.axis_index("lat")
    bands = out_ref.shape[0]
    size = bands * 8
    for half in range(2):
        for i in range(HALF // 2):
            pair = [half_rows(pix_ref, half, 2 * i + k, 4 * COLS) for k in range(2)]
            rows_s[half * size : half * size + size, 384 * i : 384 * i + 384] = jnp.concatenate(
                pair, axis=1
            ).astype(BF)
    move.wait()
    for n in range(3):
        lanes = slice(384 * n, 384 * n + 384)
        block = dot(rows_s[...], main_s[:, lanes])
        if n == 2:
            halo = dot(halo_ref[: 2 * size, :], edge_ref[...])
            block = jnp.concatenate([block[:, :256], block[:, 256:] + halo], axis=1)
        for half in range(2):
            part = block[half * size : half * size + size].reshape(bands, 8, 384).astype(BF)
            store_half(out_ref, half, lat, lanes, part)


def prepare_kernel(
    idx_ref,
    mix_ref,
    wown_ref,
    woth_ref,
    cot_ref,
    ahead_ref,
    halo_ref,
    corner_ref,
    tok_ref,
    wproj_ref,
    lw_ref,
    gb_ref,
    ga_ref,
):
    start = halo_ref.shape[0] - 4 * STRIP
    east = jnp.concatenate(
        [halo_ref[start + STRIP * t : start + STRIP * t + STRIP, :] for t in range(4)], axis=1
    )
    sides = jnp.concatenate([east, corner_ref[...], jnp.zeros((128 - 2 * STRIP, D), BF)], axis=0)
    gb = dot(tok_ref[:, :PATCHES], cot_ref[HALF:].reshape(PATCHES, D))
    gb = gb + dot(tok_ref[:, PATCHES:TOKENS], ahead_ref[...].reshape(PATCHES, D))
    gb = gb + dot(tok_ref[:, TOKENS:], sides)
    gb_ref[...] = gb.astype(BF)
    ga_ref[...] = dot(gb_ref[...], wproj_ref[...], NT).astype(BF)
    lane = lax.broadcasted_iota(jnp.int32, (256, 512), 1)
    for b in range(PSIDE):
        at = slice(256 * b, 256 * b + 256)
        idx = idx_ref[at, :]
        weight = dot(jnp.where(lane == idx, 1.0, 0.0).astype(BF), wown_ref[...])
        weight = weight + dot(jnp.where(lane + 512 == idx, 1.0, 0.0).astype(BF), woth_ref[...])
        for level in range(LEVELS):
            lw_ref[at, level * D : level * D + D] = (
                weight * mix_ref[:, level : level + 1]
            ).astype(BF)


def block_kernel(
    recv_ref,
    idxr_ref,
    mix_ref,
    gain_ref,
    mcol_ref,
    mrow_ref,
    pmain_ref,
    prest_ref,
    lw_far,
    wqkv_far,
    gb_far,
    ga_far,
    wproj_far,
    tokt_far,
    top_far,
    bot_far,
    side_top_ref,
    side_bot_ref,
    gown_far,
    goth_far,
    lw_ref,
    wqkv_ref,
    gb_ref,
    ga_ref,
    wproj_ref,
    tokt_ref,
    top_ref,
    bot_ref,
    g_ref,
    a_s,
    at_s,
    t_s,
    unit_s,
    inv_s,
    norm_s,
    qkv_s,
    att_s,
    gp_s,
    bo_s,
    gt_s,
    gs_s,
    sem_in,
    sem_out,
):
    far = [lw_far, wqkv_far, gb_far, ga_far, wproj_far, tokt_far]
    near = [lw_ref, wqkv_ref, gb_ref, ga_ref, wproj_ref, tokt_ref]
    moves = [pltpu.make_async_copy(x, y, sem_in.at[i]) for i, (x, y) in enumerate(zip(far, near))]
    for move in moves:
        move.start()
    sent = []

    def send(source, target):
        move = pltpu.make_async_copy(source, target, sem_out.at[len(sent)])
        move.start()
        sent.append(move)

    lat = lax.axis_index("lat")
    core = lax.axis_index("core")
    gain = gain_ref[...]

    halves = []
    for half in range(2):
        src = lat if half == 0 else 1 - lat
        part = recv_ref[:, src].astype(F32)
        halves.append(part.reshape(256, LANES).astype(BF))
    for b in range(PSIDE):
        place = []
        pixels = []
        for half in range(2):
            place += [pmain_ref[half], prest_ref[half, b]]
            pixels += [halves[half][:, 256 * b : 256 * b + 256], halves[half][:, 1024:1152]]
        place = jnp.concatenate(place, axis=1)
        pixels = jnp.concatenate(pixels, axis=1)
        a_s[:, 256 * b : 256 * b + 256] = dot(place, pixels, NT).astype(BF)
        at_s[256 * b : 256 * b + 256, :] = dot(pixels, place, NT).astype(BF)
    moves[0].wait()
    for level in range(LEVELS):
        tok = dot(a_s[...], lw_ref[:, level * D : level * D + D]).astype(BF).astype(F32)
        for w in range(WINDOWS):
            t_s[w * WTOK + level * 72 : w * WTOK + level * 72 + 72, :] = tok[w * 72 : w * 72 + 72]

    def norm_step(w, carry):
        rows = pl.ds(pl.multiple_of(w * WTOK, WTOK), WTOK)
        x = t_s[rows, :]
        centred = x - jnp.mean(x, axis=-1, keepdims=True)
        inv = lax.rsqrt(jnp.mean(centred * centred, axis=-1, keepdims=True) + EPS)
        unit = centred * inv
        unit_s[rows, :] = unit
        inv_s[rows, :] = inv
        norm_s[rows, :] = (unit * gain).astype(BF)
        return carry

    lax.fori_loop(0, WINDOWS, norm_step, 0)
    moves[1].wait()
    for n in range(3):
        qkv_s[:, n * D : n * D + D] = dot(norm_s[...], wqkv_ref[:, n * D : n * D + D]).astype(BF)

    for move in moves[2:]:
        move.wait()
    low = lax.broadcasted_iota(jnp.int32, (1, 128), 1) < HDIM
    lane = lax.broadcasted_iota(jnp.int32, (1, 256), 1) // HDIM
    keep = [jnp.where(lane == e, 1.0, 0.0).astype(BF) for e in range(4)]

    def by_head(x):
        return jnp.concatenate([x * keep[e] for e in range(4)], axis=0)

    def own_heads(x):
        left = jnp.where(low, x[:WTOK, :128], x[WTOK : 2 * WTOK, :128])
        right = jnp.where(low, x[2 * WTOK : 3 * WTOK, 128:], x[3 * WTOK :, 128:])
        return jnp.concatenate([left, right], axis=1).astype(BF)

    def window_step(w, carry):
        rows = pl.ds(pl.multiple_of(w * WTOK, WTOK), WTOK)
        same = mcol_ref[w] == mrow_ref[w]
        state = []
        for part in range(2):
            at = part * 256
            keys = qkv_s[rows, D + at : D + at + 256]
            values = qkv_s[rows, 2 * D + at : 2 * D + at + 256]
            queries = by_head(qkv_s[rows, at : at + 256] * 0.125)
            grads = by_head(ga_ref[rows, at : at + 256])
            state.append((keys, values, queries, grads, dot(keys, queries, NT), dot(values, grads, NT)))
        ready = []
        for keys, values, queries, grads, score, gprob in state:
            score = jnp.where(same, score, -1e30)
            ex = jnp.exp(score - jnp.max(score, axis=0, keepdims=True))
            prob = ex * (1.0 / jnp.sum(ex, axis=0, keepdims=True))
            centred = gprob - jnp.sum(prob * gprob, axis=0, keepdims=True)
            ready.append(((prob * centred).astype(BF), prob.astype(BF)))
        for part in range(2):
            at = part * 256
            keys, values, queries, grads = state[part][:4]
            gscore, prob = ready[part]
            att_s[rows, at : at + 256] = own_heads(dot(prob, values, TN))
            gp_s[rows, at : at + 256] = own_heads(dot(gscore, keys * 0.125, TN))
            gp_s[rows, D + at : D + at + 256] = dot(gscore, queries).astype(BF)
            gp_s[rows, 2 * D + at : 2 * D + at + 256] = dot(prob, grads).astype(BF)
        return carry

    lax.fori_loop(0, WINDOWS, window_step, 0)

    branch = dot(att_s[...], wproj_ref[...]).astype(BF).astype(F32)
    bo_s[...] = (t_s[...] + branch).astype(BF)
    top_ref[...] = dot(tokt_ref[:PATCHES], bo_s[...]).astype(BF)
    bot_ref[...] = dot(tokt_ref[PATCHES:TOKENS], bo_s[...]).astype(BF)
    send(top_ref, top_far)
    send(bot_ref, bot_far)
    sides = dot(tokt_ref[TOKENS:], bo_s[...]).astype(BF)
    side_top_ref[...] = sides[:STRIP]
    side_bot_ref[...] = sides[STRIP : 2 * STRIP]

    total = dot(norm_s[...], gp_s[...], TN)
    for part in range(2):
        g_ref[core ^ part, :, 0:768] = total[:, 768 * part : 768 * part + 768].astype(BF)
    total = dot(att_s[...], gb_ref[...], TN)
    for part in range(2):
        g_ref[core ^ part, :, 768:1024] = total[:, 256 * part : 256 * part + 256].astype(BF)
    for i, target in enumerate((gown_far, goth_far)):
        send(g_ref.at[i, :, :1024], target.at[:, :1024])

    for part in range(2):
        rows = slice(part * PATCHES, part * PATCHES + PATCHES)
        h = dot(gp_s[rows, :], wqkv_ref[...], NT) * gain
        unit = unit_s[rows, :]
        shifted = inv_s[rows, :] * (
            h
            - jnp.mean(h, axis=-1, keepdims=True)
            - unit * jnp.mean(h * unit, axis=-1, keepdims=True)
        )
        total = (gb_ref[rows, :].astype(F32) + shifted.astype(BF).astype(F32)).astype(BF).astype(F32)
        for i in range(WINDOWS // 2):
            w = part * (WINDOWS // 2) + i
            for level in range(LEVELS):
                at = i * WTOK + level * 72
                gt_s[level, w * 72 : w * 72 + 72, :] = total[at : at + 72]

    grads = [gt_s[level].astype(BF) for level in range(LEVELS)]
    for b in range(PSIDE):
        slot = None
        for level in range(LEVELS):
            part = dot(at_s[256 * b : 256 * b + 256, :], grads[level])
            part = part * mix_ref[:, level : level + 1]
            slot = part if slot is None else slot + part
        gs_s[256 * b : 256 * b + 256, :] = slot.astype(BF)
    row = lax.broadcasted_iota(jnp.int32, (512, 1024), 0)
    idx = idxr_ref[...]
    for i, target in ((1, goth_far), (0, gown_far)):
        pick = jnp.where(row + 512 * i == idx, 1.0, 0.0).astype(BF)
        g_ref[i, :, 1024:1536] = dot(pick, gs_s[...]).astype(BF)
        send(g_ref.at[i, :, 1024:], target.at[:, 1024:])
    for move in sent:
        move.wait()


def shape(*dims, dtype=BF):
    return jax.ShapeDtypeStruct(dims, dtype)


def cost(us):
    return pl.CostEstimate(flops=int(us * 1e9), bytes_accessed=0, transcendentals=0)


def vmem_call(kernel, outs, scratch=(), count=0, far=(), far_out=(), mib=58, us=1):
    def spec(is_far):
        return pl.BlockSpec(memory_space=pl.ANY if is_far else pltpu.VMEM)

    many = isinstance(outs, (list, tuple))
    return pl.pallas_call(
        kernel,
        out_shape=outs,
        in_specs=[spec(i in far) for i in range(count)],
        out_specs=[spec(i in far_out) for i in range(len(outs))] if many else spec(False),
        scratch_shapes=list(scratch),
        compiler_params=pltpu.CompilerParams(vmem_limit_bytes=mib * 1024 * 1024),
        cost_estimate=cost(us),
    )


def per_device(
    counts,
    pixels,
    var_order,
    embed_weight,
    level_mix,
    norm_gain,
    w_qkv,
    w_proj,
    mask_ids,
    cotangent,
):
    chips, lats, lons = counts
    bands = chips * 2
    lat = lax.axis_index("lat")
    core = lax.axis_index("core")
    lon = lax.axis_index("lon")
    rows_ring = ("chip", "core", "lat")
    everyone = ("chip", "core", "lat", "lon")
    ring = bands * lats
    group = ("chip", "lat", "lon")
    group_size = chips * lats * lons

    swap_lon = [(0, 1), (1, 0)]
    swap_core = [(0, 1), (1, 0)]

    main, edge = pixel_place()
    border, ahead, corner, copies = vmem_call(
        edge_kernel,
        [
            shape(2 * bands * 8 + 4 * STRIP, 128),
            shape(HALF, LEVELS, COLS, D),
            shape(STRIP, D),
            shape(chips, 32, D),
        ],
        count=5,
        us=3,
    )(
        pixels,
        cotangent,
        embed_weight.reshape(32, D),
        jnp.asarray(edge_place(), BF),
        jnp.asarray(strip_place(), BF),
    )
    halo = lax.ppermute(border, "lon", swap_lon)
    ahead = lax.ppermute(ahead, rows_ring, [(i, (i - 1) % ring) for i in range(ring)])
    corner = lax.ppermute(
        corner,
        everyone,
        [(i * 2 + k, ((i - 1) % ring) * 2 + 1 - k) for i in range(ring) for k in range(2)],
    )
    own_weight = lax.all_to_all(copies, "chip", split_axis=0, concat_axis=0, tiled=True)
    own_weight = own_weight.reshape(512, D)
    oth_weight = lax.ppermute(own_weight, "core", swap_core)

    packed = vmem_call(
        pack_kernel,
        shape(bands, 2, 8, LANES),
        [
            pltpu.VMEM((2 * bands * 8, LANES), BF),
            pltpu.VMEM((LANES, LANES), BF),
            pltpu.SemaphoreType.DMA,
        ],
        count=4,
        far=(3,),
        us=6,
    )(pixels, jnp.asarray(edge, BF), halo, jnp.asarray(main, BF))
    packed, ahead, corner = lax.optimization_barrier((packed, ahead, corner))
    recv = lax.all_to_all(
        packed.reshape(bands * 2, 8, LANES), rows_ring, split_axis=0, concat_axis=0, tiled=True
    ).reshape(bands, 2, 8, LANES)

    device = var_order // 2
    base = jnp.where(device % 2 == core, 0, 512) + (device // 2) * 32 + (var_order % 2) * 16
    index = base[None, :, None] + (
        jnp.arange(4)[:, None, None] + 4 * jnp.arange(4)[None, None, :]
    )
    index = index.reshape(1024).astype(jnp.int32)
    slot_mix = jnp.repeat(level_mix[var_order], 4, axis=0)

    ids = mask_ids.reshape(2, HALF, LEVELS, WINDOWS, WCOL).transpose(3, 2, 0, 1, 4)
    ids = ids.reshape(WINDOWS, WTOK)

    tok = token_place()
    level_weight, grad_branch, grad_attended = vmem_call(
        prepare_kernel, [shape(1024, 1024), shape(TOKENS, D), shape(TOKENS, D)], count=10, us=8
    )(
        index[:, None],
        slot_mix,
        own_weight,
        oth_weight,
        cotangent,
        ahead,
        halo,
        corner,
        jnp.asarray(tok, BF),
        w_proj,
    )

    pmain, prest = patch_place()
    top, bot, side_top, side_bot, gown, goth = vmem_call(
        block_kernel,
        [
            shape(PATCHES, D),
            shape(PATCHES, D),
            shape(STRIP, D),
            shape(STRIP, D),
            shape(512, 1536),
            shape(512, 1536),
        ],
        [
            pltpu.VMEM((1024, 1024), BF),
            pltpu.VMEM((D, 3 * D), BF),
            pltpu.VMEM((TOKENS, D), BF),
            pltpu.VMEM((TOKENS, D), BF),
            pltpu.VMEM((D, D), BF),
            pltpu.VMEM((TOKENS + 128, TOKENS), BF),
            pltpu.VMEM((PATCHES, D), BF),
            pltpu.VMEM((PATCHES, D), BF),
            pltpu.VMEM((2, 512, 1536), BF),
            pltpu.VMEM((PATCHES, 1024), BF),
            pltpu.VMEM((1024, PATCHES), BF),
            pltpu.VMEM((TOKENS, D), F32),
            pltpu.VMEM((TOKENS, D), F32),
            pltpu.VMEM((TOKENS, 1), F32),
            pltpu.VMEM((TOKENS, D), BF),
            pltpu.VMEM((TOKENS, 3 * D), BF),
            pltpu.VMEM((TOKENS, D), BF),
            pltpu.VMEM((TOKENS, 3 * D), BF),
            pltpu.VMEM((TOKENS, D), BF),
            pltpu.VMEM((LEVELS, PATCHES, D), F32),
            pltpu.VMEM((1024, D), BF),
            pltpu.SemaphoreType.DMA((6,)),
            pltpu.SemaphoreType.DMA((6,)),
        ],
        count=14,
        far=range(8, 14),
        far_out=(0, 1, 4, 5),
        us=38,
    )(
        recv,
        index[None, :],
        slot_mix,
        norm_gain[None, :],
        ids[:, :, None],
        jnp.tile(ids, (1, 4))[:, None, :],
        jnp.asarray(pmain, BF),
        jnp.asarray(prest, BF),
        level_weight,
        w_qkv,
        grad_branch,
        grad_attended,
        w_proj,
        jnp.asarray(tok.T, BF),
    )

    from_core = lax.ppermute(goth, "core", swap_core)
    chip_sum = (gown.astype(F32) + from_core.astype(F32)).astype(BF)
    terms = lax.all_to_all(
        chip_sum.reshape(group_size, 8, 1536), group, split_axis=0, concat_axis=0, tiled=True
    )
    owned = jnp.sum(terms.astype(F32), axis=0).astype(BF)
    copies = jnp.broadcast_to(owned[None, :, :1024], (group_size, 8, 1024))
    mine = lax.all_to_all(copies, group, split_axis=0, concat_axis=0, tiled=True)
    mine = mine.reshape(512, 1024)

    embed_part = owned[:, 1024:]
    pieces = [embed_part]
    for dlat, dlon in ((0, 1), (1, 0), (1, 1)):
        pieces.append(
            lax.ppermute(
                embed_part,
                ("lat", "lon"),
                [(i * 2 + k, (i ^ dlat) * 2 + (k ^ dlon)) for i in range(2) for k in range(2)],
            )
        )
    stacked = jnp.stack(pieces)
    tile = lat * 2 + lon
    grad_embed = jnp.concatenate(
        [lax.dynamic_index_in_dim(stacked, tile ^ t, 0, keepdims=False) for t in range(4)], axis=0
    )
    grad_embed = grad_embed.reshape(2, 16, D).astype(F32)

    from_before = lax.ppermute(bot, rows_ring, [(i, (i + 1) % ring) for i in range(ring)])
    west = lax.ppermute(side_top, "lon", swap_lon)
    south_west = lax.ppermute(
        side_bot,
        everyone,
        [(i * 2 + k, ((i + 1) % ring) * 2 + 1 - k) for i in range(ring) for k in range(2)],
    )
    _, from_before, west, south_west = lax.optimization_barrier((owned, from_before, west, south_west))
    body = jnp.concatenate([from_before, top], axis=0).reshape(ROWS, LEVELS, COLS, D)
    sides = jnp.concatenate([south_west[:36], west[:36]], axis=0).reshape(ROWS, LEVELS, 3, D)
    block_out = jnp.concatenate([sides, body[:, :, 3:]], axis=2)

    mine, block_out, grad_embed = lax.optimization_barrier((mine, block_out, grad_embed))
    other = lax.ppermute(mine, "core", swap_core)
    grads = []
    for lanes, width in ((slice(0, 768), 768), (slice(768, 1024), 256)):
        own = jnp.concatenate([mine[:, lanes]] * 2, axis=1).astype(F32)
        rest = other[:, lanes].astype(F32)
        grads.append(lax.dynamic_update_slice(own, rest, (0, (1 - core) * width)))
    grad_qkv, grad_proj = grads
    return (block_out, grad_embed, grad_qkv, grad_proj)


def solution(mesh):
    var, lats, lons = (mesh.shape[name] for name in ("var", "lat", "lon"))
    chips = var // 2
    fine = Mesh(mesh.devices.reshape(chips, 2, lats, lons), ("chip", "core", "lat", "lon"))
    both = ("chip", "core")
    in_specs = (
        P(None, "lat", both, None, "lon"),
        P(),
        P(both, None, None),
        P(),
        P(),
        P(),
        P(),
        P(("chip", "core", "lat"), None, "lon"),
        P(("chip", "core", "lat"), None, "lon", None),
    )
    out_specs = (P(("chip", "core", "lat"), None, "lon", None), P(both, None, None), P(), P())
    return jax.shard_map(
        functools.partial(per_device, (chips, lats, lons)),
        mesh=fine,
        in_specs=in_specs,
        out_specs=out_specs,
        check_vma=False,
    )
```

```python
import functools

import jax
import jax.numpy as jnp
import numpy as np
from jax import lax
from jax.experimental import pallas as pl
from jax.experimental.pallas import tpu as pltpu
from jax.sharding import Mesh, PartitionSpec as P

D = 512
HEADS = 8
HDIM = 64
PSIDE = 4
WCOL = 6
ROWS = 12
HALF = 6
COLS = 48
WINDOWS = 8
LEVELS = 2
TOKENS = 1152
WTOK = 144
PATCHES = 576
LANES = 1152
STRIP = 48
EPS = 1e-05
BF = jnp.bfloat16
F32 = jnp.float32

NN = (((1,), (0,)), ((), ()))
NT = (((1,), (1,)), ((), ()))
TN = (((0,), (0,)), ((), ()))


def dot(a, b, dims=NN):
    return lax.dot_general(a, b, dims, preferred_element_type=F32)


def patch_index(w, j, c6):
    if w == WINDOWS - 1:
        return 252 + j * 3 + c6 if c6 < 3 else 267 + j * 3 + c6
    return w * 36 + j * WCOL + c6


def pixel_lane(b, patch):
    return 256 * b + patch if patch < 256 else 1024 + 32 * b + patch - 256


def edge_place():
    place = np.zeros((HALF, 128, 128), np.float32)
    for j in range(HALF):
        lane = np.arange(12)
        place[j, lane, j * 12 + lane] = 1
    return place


def pixel_place():
    main = np.zeros((HALF * PSIDE * COLS, LANES), np.float32)
    edge = np.zeros((128, 128), np.float32)
    for j in range(HALF):
        for c in range(COLS):
            for b in range(PSIDE):
                col = c - 3 if c >= 3 else COLS - 3 + c
                lane = pixel_lane(b, patch_index(col // WCOL, j, col % WCOL))
                if c >= 3:
                    main[(j * COLS + c) * PSIDE + b, lane] = 1
                else:
                    edge[j * 12 + c * PSIDE + b, lane - 1024] = 1
    return main, edge


def patch_place():
    main = np.zeros((2, PATCHES, 256), np.float32)
    rest = np.zeros((2, PSIDE, PATCHES, 128), np.float32)
    for half in range(2):
        for w in range(WINDOWS):
            for i in range(36):
                patch = patch_index(w, i // WCOL, i % WCOL)
                row = w * 72 + half * 36 + i
                if patch < 256:
                    main[half, row, patch] = 1
                else:
                    for b in range(PSIDE):
                        rest[half, b, row, 32 * b + patch - 256] = 1
    return main, rest


def token_place():
    place = np.zeros((TOKENS, TOKENS + 128), np.float32)
    for w in range(WINDOWS):
        for level in range(LEVELS):
            for half in range(2):
                for j in range(HALF):
                    for c6 in range(WCOL):
                        t = w * WTOK + level * 72 + half * 36 + j * WCOL + c6
                        c = w * WCOL + c6 + 3
                        if c < COLS:
                            place[t, half * PATCHES + (j * LEVELS + level) * COLS + c] = 1
                        else:
                            place[t, TOKENS + half * STRIP + (j * LEVELS + level) * 3 + c - COLS] = 1
    return place


def half_rows(pix_ref, half, j, lanes):
    rows = pix_ref[:, half * HALF + j, :, :, :lanes].astype(F32)
    merged = jnp.concatenate([rows[:, 0], rows[:, 1]], axis=1)
    return merged.reshape(merged.shape[0] * 8, lanes)


def strip_place():
    place = np.zeros((2 * STRIP, ROWS * LEVELS * 16), np.float32)
    for half in range(2):
        for i in range(HALF * LEVELS):
            for c in range(3):
                place[half * STRIP + i * 3 + c, (half * HALF * LEVELS + i) * 16 + c] = 1
    return place


def edge_kernel(
    pix_ref, cot_ref, weight_ref, place_ref, strip_ref, west_ref, ahead_ref, corner_ref, copies_ref
):
    size = (west_ref.shape[0] - 4 * STRIP) // 2
    for half in range(2):
        total = None
        for j in range(HALF):
            term = dot(half_rows(pix_ref, half, j, 128).astype(BF), place_ref[j])
            total = term if total is None else total + term
        west_ref[half * size : half * size + size, :] = total.astype(BF)
    strips = cot_ref[:, :, :16, :].reshape(ROWS * LEVELS * 16, D)
    strips = dot(strip_ref[...], strips).astype(BF)
    corner_ref[...] = strips[:STRIP]
    for t in range(4):
        at = 2 * size + t * STRIP
        west_ref[at : at + STRIP, :] = strips[STRIP:, 128 * t : 128 * t + 128]
    ahead_ref[...] = cot_ref[:HALF]
    copies_ref[...] = jnp.broadcast_to(weight_ref[...][None], copies_ref.shape)


def store_half(out_ref, half, lat, lanes, block):
    bands = out_ref.shape[0]
    if half == 1:
        out_ref[:, lat, :, lanes] = block
        return

    @pl.when(lat == 0)
    def _():
        out_ref[: bands - 1, 1, :, lanes] = block[1:]
        out_ref[bands - 1 :, 1, :, lanes] = block[:1]

    @pl.when(lat == 1)
    def _():
        out_ref[:, 0, :, lanes] = block


def pack_kernel(pix_ref, edge_ref, halo_ref, main_ref, out_ref, rows_s, main_s, sem):
    move = pltpu.make_async_copy(main_ref, main_s, sem)
    move.start()
    lat = lax.axis_index("lat")
    bands = out_ref.shape[0]
    size = bands * 8
    for half in range(2):
        for i in range(HALF // 2):
            pair = [half_rows(pix_ref, half, 2 * i + k, 4 * COLS) for k in range(2)]
            rows_s[half * size : half * size + size, 384 * i : 384 * i + 384] = jnp.concatenate(
                pair, axis=1
            ).astype(BF)
    move.wait()
    for n in range(3):
        lanes = slice(384 * n, 384 * n + 384)
        block = dot(rows_s[...], main_s[:, lanes])
        if n == 2:
            halo = dot(halo_ref[: 2 * size, :], edge_ref[...])
            block = jnp.concatenate([block[:, :256], block[:, 256:] + halo], axis=1)
        for half in range(2):
            part = block[half * size : half * size + size].reshape(bands, 8, 384).astype(BF)
            store_half(out_ref, half, lat, lanes, part)


def prepare_kernel(
    idx_ref,
    mix_ref,
    wown_ref,
    woth_ref,
    cot_ref,
    ahead_ref,
    halo_ref,
    corner_ref,
    tok_ref,
    wproj_ref,
    lw_ref,
    gb_ref,
    ga_ref,
):
    start = halo_ref.shape[0] - 4 * STRIP
    east = jnp.concatenate(
        [halo_ref[start + STRIP * t : start + STRIP * t + STRIP, :] for t in range(4)], axis=1
    )
    sides = jnp.concatenate([east, corner_ref[...], jnp.zeros((128 - 2 * STRIP, D), BF)], axis=0)
    gb = dot(tok_ref[:, :PATCHES], cot_ref[HALF:].reshape(PATCHES, D))
    gb = gb + dot(tok_ref[:, PATCHES:TOKENS], ahead_ref[...].reshape(PATCHES, D))
    gb = gb + dot(tok_ref[:, TOKENS:], sides)
    gb_ref[...] = gb.astype(BF)
    ga_ref[...] = dot(gb_ref[...], wproj_ref[...], NT).astype(BF)
    lane = lax.broadcasted_iota(jnp.int32, (256, 512), 1)
    for b in range(PSIDE):
        at = slice(256 * b, 256 * b + 256)
        idx = idx_ref[at, :]
        weight = dot(jnp.where(lane == idx, 1.0, 0.0).astype(BF), wown_ref[...])
        weight = weight + dot(jnp.where(lane + 512 == idx, 1.0, 0.0).astype(BF), woth_ref[...])
        for level in range(LEVELS):
            lw_ref[at, level * D : level * D + D] = (
                weight * mix_ref[:, level : level + 1]
            ).astype(BF)


def block_kernel(
    recv_ref,
    idxr_ref,
    mix_ref,
    gain_ref,
    mcol_ref,
    mrow_ref,
    pmain_ref,
    prest_ref,
    lw_far,
    wqkv_far,
    gb_far,
    ga_far,
    tok_far,
    att_far,
    gown_far,
    goth_far,
    lw_ref,
    wqkv_ref,
    gb_ref,
    ga_ref,
    g_ref,
    a_s,
    at_s,
    t_s,
    unit_s,
    inv_s,
    norm_s,
    qkv_s,
    att_s,
    gp_s,
    bo_s,
    gt_s,
    gs_s,
    sem_in,
    sem_out,
):
    far = [lw_far, wqkv_far, gb_far, ga_far]
    near = [lw_ref, wqkv_ref, gb_ref, ga_ref]
    moves = [pltpu.make_async_copy(x, y, sem_in.at[i]) for i, (x, y) in enumerate(zip(far, near))]
    for move in moves:
        move.start()
    sent = []

    def send(source, target):
        move = pltpu.make_async_copy(source, target, sem_out.at[len(sent)])
        move.start()
        sent.append(move)

    lat = lax.axis_index("lat")
    core = lax.axis_index("core")
    gain = gain_ref[...]

    halves = []
    for half in range(2):
        src = lat if half == 0 else 1 - lat
        part = recv_ref[:, src].astype(F32)
        halves.append(part.reshape(256, LANES).astype(BF))
    for b in range(PSIDE):
        place = []
        pixels = []
        for half in range(2):
            place += [pmain_ref[half], prest_ref[half, b]]
            pixels += [halves[half][:, 256 * b : 256 * b + 256], halves[half][:, 1024:1152]]
        place = jnp.concatenate(place, axis=1)
        pixels = jnp.concatenate(pixels, axis=1)
        a_s[:, 256 * b : 256 * b + 256] = dot(place, pixels, NT).astype(BF)
        at_s[256 * b : 256 * b + 256, :] = dot(pixels, place, NT).astype(BF)
    moves[0].wait()
    for level in range(LEVELS):
        tok = dot(a_s[...], lw_ref[:, level * D : level * D + D]).astype(BF).astype(F32)
        for w in range(WINDOWS):
            t_s[w * WTOK + level * 72 : w * WTOK + level * 72 + 72, :] = tok[w * 72 : w * 72 + 72]

    bo_s[...] = t_s[...].astype(BF)
    send(bo_s, tok_far)

    def norm_step(w, carry):
        rows = pl.ds(pl.multiple_of(w * WTOK, WTOK), WTOK)
        x = t_s[rows, :]
        centred = x - jnp.mean(x, axis=-1, keepdims=True)
        inv = lax.rsqrt(jnp.mean(centred * centred, axis=-1, keepdims=True) + EPS)
        unit = centred * inv
        unit_s[rows, :] = unit
        inv_s[rows, :] = inv
        norm_s[rows, :] = (unit * gain).astype(BF)
        return carry

    lax.fori_loop(0, WINDOWS, norm_step, 0, unroll=True)
    moves[1].wait()
    for n in range(3):
        qkv_s[:, n * D : n * D + D] = dot(norm_s[...], wqkv_ref[:, n * D : n * D + D]).astype(BF)

    for move in moves[2:]:
        move.wait()
    low = lax.broadcasted_iota(jnp.int32, (1, 128), 1) < HDIM
    lane = lax.broadcasted_iota(jnp.int32, (1, 256), 1) // HDIM
    keep = [jnp.where(lane == e, 1.0, 0.0).astype(BF) for e in range(4)]

    def by_head(x):
        return jnp.concatenate([x * keep[e] for e in range(4)], axis=0)

    def own_heads(x):
        left = jnp.where(low, x[:WTOK, :128], x[WTOK : 2 * WTOK, :128])
        right = jnp.where(low, x[2 * WTOK : 3 * WTOK, 128:], x[3 * WTOK :, 128:])
        return jnp.concatenate([left, right], axis=1).astype(BF)

    def window_step(w, carry):
        rows = pl.ds(pl.multiple_of(w * WTOK, WTOK), WTOK)
        same = mcol_ref[w] == mrow_ref[w]
        state = []
        for part in range(2):
            at = part * 256
            keys = qkv_s[rows, D + at : D + at + 256]
            values = qkv_s[rows, 2 * D + at : 2 * D + at + 256]
            queries = by_head(qkv_s[rows, at : at + 256] * 0.125)
            grads = by_head(ga_ref[rows, at : at + 256])
            state.append((keys, values, queries, grads, dot(keys, queries, NT), dot(values, grads, NT)))
        ready = []
        for keys, values, queries, grads, score, gprob in state:
            score = jnp.where(same, score, -1e30)
            ex = jnp.exp(score - jnp.max(score, axis=0, keepdims=True))
            prob = ex * (1.0 / jnp.sum(ex, axis=0, keepdims=True))
            centred = gprob - jnp.sum(prob * gprob, axis=0, keepdims=True)
            ready.append(((prob * centred).astype(BF), prob.astype(BF)))
        for part in range(2):
            at = part * 256
            keys, values, queries, grads = state[part][:4]
            gscore, prob = ready[part]
            att_s[rows, at : at + 256] = own_heads(dot(prob, values, TN))
            gp_s[rows, at : at + 256] = own_heads(dot(gscore, keys * 0.125, TN))
            gp_s[rows, D + at : D + at + 256] = dot(gscore, queries).astype(BF)
            gp_s[rows, 2 * D + at : 2 * D + at + 256] = dot(prob, grads).astype(BF)
        return carry

    lax.fori_loop(0, WINDOWS, window_step, 0, unroll=4)

    send(att_s, att_far)

    total = dot(norm_s[...], gp_s[...], TN)
    for part in range(2):
        g_ref[core ^ part, :, 0:768] = total[:, 768 * part : 768 * part + 768].astype(BF)
    total = dot(att_s[...], gb_ref[...], TN)
    for part in range(2):
        g_ref[core ^ part, :, 768:1024] = total[:, 256 * part : 256 * part + 256].astype(BF)
    for i, target in enumerate((gown_far, goth_far)):
        send(g_ref.at[i, :, :1024], target.at[:, :1024])

    for part in range(2):
        rows = slice(part * PATCHES, part * PATCHES + PATCHES)
        h = dot(gp_s[rows, :], wqkv_ref[...], NT) * gain
        unit = unit_s[rows, :]
        shifted = inv_s[rows, :] * (
            h
            - jnp.mean(h, axis=-1, keepdims=True)
            - unit * jnp.mean(h * unit, axis=-1, keepdims=True)
        )
        total = (gb_ref[rows, :].astype(F32) + shifted.astype(BF).astype(F32)).astype(BF).astype(F32)
        for i in range(WINDOWS // 2):
            w = part * (WINDOWS // 2) + i
            for level in range(LEVELS):
                at = i * WTOK + level * 72
                gt_s[level, w * 72 : w * 72 + 72, :] = total[at : at + 72]

    grads = [gt_s[level].astype(BF) for level in range(LEVELS)]
    for b in range(PSIDE):
        slot = None
        for level in range(LEVELS):
            part = dot(at_s[256 * b : 256 * b + 256, :], grads[level])
            part = part * mix_ref[:, level : level + 1]
            slot = part if slot is None else slot + part
        gs_s[256 * b : 256 * b + 256, :] = slot.astype(BF)
    row = lax.broadcasted_iota(jnp.int32, (512, 1024), 0)
    idx = idxr_ref[...]
    for i, target in ((1, goth_far), (0, gown_far)):
        pick = jnp.where(row + 512 * i == idx, 1.0, 0.0).astype(BF)
        g_ref[i, :, 1024:1536] = dot(pick, gs_s[...]).astype(BF)
        send(g_ref.at[i, :, 1024:], target.at[:, 1024:])
    for move in sent:
        move.wait()


def out_kernel(tok_ref, att_ref, wproj_ref, tokt_ref, top_ref, bot_ref, side_top_ref, side_bot_ref):
    branch = dot(att_ref[...], wproj_ref[...]).astype(BF).astype(F32)
    total = (tok_ref[...].astype(F32) + branch).astype(BF)
    top_ref[...] = dot(tokt_ref[:PATCHES], total).astype(BF)
    bot_ref[...] = dot(tokt_ref[PATCHES:TOKENS], total).astype(BF)
    sides = dot(tokt_ref[TOKENS:], total).astype(BF)
    side_top_ref[...] = sides[:STRIP]
    side_bot_ref[...] = sides[STRIP : 2 * STRIP]


def add_kernel(left_ref, right_ref, out_ref):
    out_ref[...] = (left_ref[...].astype(F32) + right_ref[...].astype(F32)).astype(BF)


def join_kernel(mine_ref, other_ref, qkv_far, proj_far, qkv_s, proj_s, sems):
    core = lax.axis_index("core")
    moves = []
    for i, ref in enumerate((mine_ref, other_ref)):
        for near, far, lanes in ((qkv_s, qkv_far, slice(0, 768)), (proj_s, proj_far, slice(768, 1024))):
            width = near.shape[2]
            near[i] = ref[:, lanes].astype(F32)
            at = pl.multiple_of((core ^ i) * width, 256)
            move = pltpu.make_async_copy(near.at[i], far.at[:, pl.ds(at, width)], sems.at[len(moves)])
            move.start()
            moves.append(move)
    for move in moves:
        move.wait()


def shape(*dims, dtype=BF):
    return jax.ShapeDtypeStruct(dims, dtype)


def cost(us):
    return pl.CostEstimate(flops=int(us * 1e9), bytes_accessed=0, transcendentals=0)


def vmem_call(kernel, outs, scratch=(), count=0, far=(), far_out=(), mib=58, us=1):
    def spec(is_far):
        return pl.BlockSpec(memory_space=pl.ANY if is_far else pltpu.VMEM)

    many = isinstance(outs, (list, tuple))
    return pl.pallas_call(
        kernel,
        out_shape=outs,
        in_specs=[spec(i in far) for i in range(count)],
        out_specs=[spec(i in far_out) for i in range(len(outs))] if many else spec(False),
        scratch_shapes=list(scratch),
        compiler_params=pltpu.CompilerParams(vmem_limit_bytes=mib * 1024 * 1024),
        cost_estimate=cost(us),
    )


def per_device(
    counts,
    pixels,
    var_order,
    embed_weight,
    level_mix,
    norm_gain,
    w_qkv,
    w_proj,
    mask_ids,
    cotangent,
):
    chips, lats, lons = counts
    bands = chips * 2
    lat = lax.axis_index("lat")
    core = lax.axis_index("core")
    lon = lax.axis_index("lon")
    rows_ring = ("chip", "core", "lat")
    everyone = ("chip", "core", "lat", "lon")
    ring = bands * lats
    group = ("chip", "lat", "lon")
    group_size = chips * lats * lons

    swap_lon = [(0, 1), (1, 0)]
    swap_core = [(0, 1), (1, 0)]

    main, edge = pixel_place()
    border, ahead, corner, copies = vmem_call(
        edge_kernel,
        [
            shape(2 * bands * 8 + 4 * STRIP, 128),
            shape(HALF, LEVELS, COLS, D),
            shape(STRIP, D),
            shape(chips, 32, D),
        ],
        count=5,
        us=3,
    )(
        pixels,
        cotangent,
        embed_weight.reshape(32, D),
        jnp.asarray(edge_place(), BF),
        jnp.asarray(strip_place(), BF),
    )
    halo = lax.ppermute(border, "lon", swap_lon)
    halo, ahead, corner = lax.optimization_barrier((halo, ahead, corner))
    ahead = lax.ppermute(ahead, rows_ring, [(i, (i - 1) % ring) for i in range(ring)])
    corner = lax.ppermute(
        corner,
        everyone,
        [(i * 2 + k, ((i - 1) % ring) * 2 + 1 - k) for i in range(ring) for k in range(2)],
    )
    own_weight = lax.all_to_all(copies, "chip", split_axis=0, concat_axis=0, tiled=True)
    own_weight = own_weight.reshape(512, D)
    oth_weight = lax.ppermute(own_weight, "core", swap_core)

    packed = vmem_call(
        pack_kernel,
        shape(bands, 2, 8, LANES),
        [
            pltpu.VMEM((2 * bands * 8, LANES), BF),
            pltpu.VMEM((LANES, LANES), BF),
            pltpu.SemaphoreType.DMA,
        ],
        count=4,
        far=(3,),
        us=6,
    )(pixels, jnp.asarray(edge, BF), halo, jnp.asarray(main, BF))
    recv = lax.all_to_all(
        packed.reshape(bands * 2, 8, LANES), rows_ring, split_axis=0, concat_axis=0, tiled=True
    ).reshape(bands, 2, 8, LANES)

    var_order, ahead, corner = lax.optimization_barrier((var_order, ahead, corner))
    device = var_order // 2
    base = jnp.where(device % 2 == core, 0, 512) + (device // 2) * 32 + (var_order % 2) * 16
    index = base[None, :, None] + (
        jnp.arange(4)[:, None, None] + 4 * jnp.arange(4)[None, None, :]
    )
    index = index.reshape(1024).astype(jnp.int32)
    slot_mix = jnp.repeat(level_mix[var_order], 4, axis=0)

    ids = mask_ids.reshape(2, HALF, LEVELS, WINDOWS, WCOL).transpose(3, 2, 0, 1, 4)
    ids = ids.reshape(WINDOWS, WTOK)

    tok = token_place()
    level_weight, grad_branch, grad_attended = vmem_call(
        prepare_kernel, [shape(1024, 1024), shape(TOKENS, D), shape(TOKENS, D)], count=10, us=8
    )(
        index[:, None],
        slot_mix,
        own_weight,
        oth_weight,
        cotangent,
        ahead,
        halo,
        corner,
        jnp.asarray(tok, BF),
        w_proj,
    )

    pmain, prest = patch_place()
    tokens, attended, gown, goth = vmem_call(
        block_kernel,
        [
            shape(TOKENS, D),
            shape(TOKENS, D),
            shape(512, 1536),
            shape(512, 1536),
        ],
        [
            pltpu.VMEM((1024, 1024), BF),
            pltpu.VMEM((D, 3 * D), BF),
            pltpu.VMEM((TOKENS, D), BF),
            pltpu.VMEM((TOKENS, D), BF),
            pltpu.VMEM((2, 512, 1536), BF),
            pltpu.VMEM((PATCHES, 1024), BF),
            pltpu.VMEM((1024, PATCHES), BF),
            pltpu.VMEM((TOKENS, D), F32),
            pltpu.VMEM((TOKENS, D), F32),
            pltpu.VMEM((TOKENS, 1), F32),
            pltpu.VMEM((TOKENS, D), BF),
            pltpu.VMEM((TOKENS, 3 * D), BF),
            pltpu.VMEM((TOKENS, D), BF),
            pltpu.VMEM((TOKENS, 3 * D), BF),
            pltpu.VMEM((TOKENS, D), BF),
            pltpu.VMEM((LEVELS, PATCHES, D), F32),
            pltpu.VMEM((1024, D), BF),
            pltpu.SemaphoreType.DMA((4,)),
            pltpu.SemaphoreType.DMA((6,)),
        ],
        count=12,
        far=range(8, 12),
        far_out=(0, 1, 2, 3),
        us=28,
    )(
        recv,
        index[None, :],
        slot_mix,
        norm_gain[None, :],
        ids[:, :, None],
        jnp.tile(ids, (1, 4))[:, None, :],
        jnp.asarray(pmain, BF),
        jnp.asarray(prest, BF),
        level_weight,
        w_qkv,
        grad_branch,
        grad_attended,
    )

    from_core = lax.ppermute(goth, "core", swap_core)
    chip_sum = vmem_call(add_kernel, shape(512, 1536), count=2, mib=7, us=2)(gown, from_core)
    terms = lax.all_to_all(
        chip_sum.reshape(group_size, 8, 1536), group, split_axis=0, concat_axis=0, tiled=True
    )
    owned = jnp.sum(terms.astype(F32), axis=0).astype(BF)
    copies = jnp.broadcast_to(owned[None, :, :1024], (group_size, 8, 1024))
    mine = lax.all_to_all(copies, group, split_axis=0, concat_axis=0, tiled=True)
    mine = mine.reshape(512, 1024)

    embed_part = owned[:, 1024:]
    pieces = [embed_part]
    for dlat, dlon in ((0, 1), (1, 0), (1, 1)):
        pieces.append(
            lax.ppermute(
                embed_part,
                ("lat", "lon"),
                [(i * 2 + k, (i ^ dlat) * 2 + (k ^ dlon)) for i in range(2) for k in range(2)],
            )
        )
    stacked = jnp.stack(pieces)
    tile = lat * 2 + lon
    grad_embed = jnp.concatenate(
        [lax.dynamic_index_in_dim(stacked, tile ^ t, 0, keepdims=False) for t in range(4)], axis=0
    )
    grad_embed = grad_embed.reshape(2, 16, D).astype(F32)

    top, bot, side_top, side_bot = vmem_call(
        out_kernel,
        [shape(PATCHES, D), shape(PATCHES, D), shape(STRIP, D), shape(STRIP, D)],
        count=4,
        us=5,
    )(tokens, attended, w_proj, jnp.asarray(tok.T, BF))
    from_before = lax.ppermute(bot, rows_ring, [(i, (i + 1) % ring) for i in range(ring)])
    west = lax.ppermute(side_top, "lon", swap_lon)
    south_west = lax.ppermute(
        side_bot,
        everyone,
        [(i * 2 + k, ((i + 1) % ring) * 2 + 1 - k) for i in range(ring) for k in range(2)],
    )
    _, from_before, west, south_west = lax.optimization_barrier((owned, from_before, west, south_west))
    body = jnp.concatenate([from_before, top], axis=0).reshape(ROWS, LEVELS, COLS, D)
    sides = jnp.concatenate([south_west[:36], west[:36]], axis=0).reshape(ROWS, LEVELS, 3, D)
    block_out = jnp.concatenate([sides, body[:, :, 3:]], axis=2)

    mine, block_out, grad_embed = lax.optimization_barrier((mine, block_out, grad_embed))
    other = lax.ppermute(mine, "core", swap_core)
    grad_qkv, grad_proj = vmem_call(
        join_kernel,
        [shape(512, 1536, dtype=F32), shape(512, 512, dtype=F32)],
        [
            pltpu.VMEM((2, 512, 768), F32),
            pltpu.VMEM((2, 512, 256), F32),
            pltpu.SemaphoreType.DMA((4,)),
        ],
        count=2,
        far_out=(0, 1),
        mib=10,
        us=2,
    )(mine, other)
    return (block_out, grad_embed, grad_qkv, grad_proj)


def solution(mesh):
    var, lats, lons = (mesh.shape[name] for name in ("var", "lat", "lon"))
    chips = var // 2
    fine = Mesh(mesh.devices.reshape(chips, 2, lats, lons), ("chip", "core", "lat", "lon"))
    both = ("chip", "core")
    in_specs = (
        P(None, "lat", both, None, "lon"),
        P(),
        P(both, None, None),
        P(),
        P(),
        P(),
        P(),
        P(("chip", "core", "lat"), None, "lon"),
        P(("chip", "core", "lat"), None, "lon", None),
    )
    out_specs = (P(("chip", "core", "lat"), None, "lon", None), P(both, None, None), P(), P())
    return jax.shard_map(
        functools.partial(per_device, (chips, lats, lons)),
        mesh=fine,
        in_specs=in_specs,
        out_specs=out_specs,
        check_vma=False,
    )
```

```python
import functools

import jax
import jax.numpy as jnp
import numpy as np
from jax import lax
from jax.experimental import pallas as pl
from jax.experimental.pallas import tpu as pltpu
from jax.sharding import Mesh, PartitionSpec as P

D = 512
HEADS = 8
HDIM = 64
PSIDE = 4
WCOL = 6
ROWS = 12
HALF = 6
COLS = 48
WINDOWS = 8
LEVELS = 2
TOKENS = 1152
WTOK = 144
PATCHES = 576
LANES = 1152
STRIP = 48
EPS = 1e-05
BF = jnp.bfloat16
F32 = jnp.float32

NN = (((1,), (0,)), ((), ()))
NT = (((1,), (1,)), ((), ()))
TN = (((0,), (0,)), ((), ()))


def dot(a, b, dims=NN):
    return lax.dot_general(a, b, dims, preferred_element_type=F32)


def patch_index(w, j, c6):
    if w == WINDOWS - 1:
        return 252 + j * 3 + c6 if c6 < 3 else 267 + j * 3 + c6
    return w * 36 + j * WCOL + c6


def pixel_lane(b, patch):
    return 256 * b + patch if patch < 256 else 1024 + 32 * b + patch - 256


def edge_place():
    place = np.zeros((HALF, 128, 128), np.float32)
    for j in range(HALF):
        lane = np.arange(12)
        place[j, lane, j * 12 + lane] = 1
    return place


def pixel_place():
    main = np.zeros((HALF * PSIDE * COLS, LANES), np.float32)
    edge = np.zeros((128, 128), np.float32)
    for j in range(HALF):
        for c in range(COLS):
            for b in range(PSIDE):
                col = c - 3 if c >= 3 else COLS - 3 + c
                lane = pixel_lane(b, patch_index(col // WCOL, j, col % WCOL))
                if c >= 3:
                    main[(j * COLS + c) * PSIDE + b, lane] = 1
                else:
                    edge[j * 12 + c * PSIDE + b, lane - 1024] = 1
    return main, edge


def patch_place():
    main = np.zeros((2, PATCHES, 256), np.float32)
    rest = np.zeros((2, PSIDE, PATCHES, 128), np.float32)
    for half in range(2):
        for w in range(WINDOWS):
            for i in range(36):
                patch = patch_index(w, i // WCOL, i % WCOL)
                row = w * 72 + half * 36 + i
                if patch < 256:
                    main[half, row, patch] = 1
                else:
                    for b in range(PSIDE):
                        rest[half, b, row, 32 * b + patch - 256] = 1
    return main, rest


def token_place():
    place = np.zeros((TOKENS, TOKENS + 128), np.float32)
    for w in range(WINDOWS):
        for level in range(LEVELS):
            for half in range(2):
                for j in range(HALF):
                    for c6 in range(WCOL):
                        t = w * WTOK + level * 72 + half * 36 + j * WCOL + c6
                        c = w * WCOL + c6 + 3
                        if c < COLS:
                            place[t, half * PATCHES + (j * LEVELS + level) * COLS + c] = 1
                        else:
                            place[t, TOKENS + half * STRIP + (j * LEVELS + level) * 3 + c - COLS] = 1
    return place


def half_rows(pix_ref, half, j, lanes):
    rows = pix_ref[:, half * HALF + j, :, :, :lanes].astype(F32)
    merged = jnp.concatenate([rows[:, 0], rows[:, 1]], axis=1)
    return merged.reshape(merged.shape[0] * 8, lanes)


def strip_place():
    place = np.zeros((2 * STRIP, ROWS * LEVELS * 16), np.float32)
    for half in range(2):
        for i in range(HALF * LEVELS):
            for c in range(3):
                place[half * STRIP + i * 3 + c, (half * HALF * LEVELS + i) * 16 + c] = 1
    return place


def edge_kernel(
    pix_ref, cot_ref, weight_ref, place_ref, strip_ref, west_ref, ahead_ref, corner_ref, copies_ref
):
    size = (west_ref.shape[0] - 4 * STRIP) // 2
    for half in range(2):
        total = None
        for j in range(HALF):
            term = dot(half_rows(pix_ref, half, j, 128).astype(BF), place_ref[j])
            total = term if total is None else total + term
        west_ref[half * size : half * size + size, :] = total.astype(BF)
    strips = cot_ref[:, :, :16, :].reshape(ROWS * LEVELS * 16, D)
    strips = dot(strip_ref[...], strips).astype(BF)
    corner_ref[...] = strips[:STRIP]
    for t in range(4):
        at = 2 * size + t * STRIP
        west_ref[at : at + STRIP, :] = strips[STRIP:, 128 * t : 128 * t + 128]
    ahead_ref[...] = cot_ref[:HALF]
    copies_ref[...] = jnp.broadcast_to(weight_ref[...][None], copies_ref.shape)


def pack_kernel(pix_ref, edge_ref, halo_ref, main_ref, out_ref, rows_s, main_s, out_s, sems):
    move = pltpu.make_async_copy(main_ref, main_s, sems.at[0])
    move.start()
    lat = lax.axis_index("lat")
    bands = out_ref.shape[0]
    size = bands * 8
    moves = []
    for half in range(2):
        for i in range(HALF // 2):
            pair = [half_rows(pix_ref, half, 2 * i + k, 4 * COLS) for k in range(2)]
            rows_s[half, :, 384 * i : 384 * i + 384] = jnp.concatenate(pair, axis=1).astype(BF)
        if half == 0:
            move.wait()
        for n in range(3):
            lanes = slice(384 * n, 384 * n + 384)
            block = dot(rows_s[half], main_s[:, lanes])
            if n == 2:
                halo = dot(halo_ref[half * size : half * size + size, :], edge_ref[...])
                block = jnp.concatenate([block[:, :256], block[:, 256:] + halo], axis=1)
            block = block.reshape(bands, 8, 384)
            if half == 0:
                later = jnp.concatenate([block[1:], block[:1]], axis=0)
                block = jnp.where(lat == 0, later, block)
            out_s[half, :, :, lanes] = block.astype(BF)
        target = lat if half == 1 else 1 - lat
        moves.append(pltpu.make_async_copy(out_s.at[half], out_ref.at[:, target], sems.at[1 + half]))
        moves[half].start()
    for move in moves:
        move.wait()


def prepare_kernel(
    idx_ref,
    mix_ref,
    wown_ref,
    woth_ref,
    cot_ref,
    ahead_ref,
    halo_ref,
    corner_ref,
    tok_ref,
    wproj_ref,
    lw_ref,
    gb_ref,
    ga_ref,
):
    start = halo_ref.shape[0] - 4 * STRIP
    east = jnp.concatenate(
        [halo_ref[start + STRIP * t : start + STRIP * t + STRIP, :] for t in range(4)], axis=1
    )
    sides = jnp.concatenate([east, corner_ref[...], jnp.zeros((128 - 2 * STRIP, D), BF)], axis=0)
    gb = dot(tok_ref[:, :PATCHES], cot_ref[HALF:].reshape(PATCHES, D))
    gb = gb + dot(tok_ref[:, PATCHES:TOKENS], ahead_ref[...].reshape(PATCHES, D))
    gb = gb + dot(tok_ref[:, TOKENS:], sides)
    gb_ref[...] = gb.astype(BF)
    ga_ref[...] = dot(gb_ref[...], wproj_ref[...], NT).astype(BF)
    lane = lax.broadcasted_iota(jnp.int32, (256, 512), 1)
    for b in range(PSIDE):
        at = slice(256 * b, 256 * b + 256)
        idx = idx_ref[at, :]
        weight = dot(jnp.where(lane == idx, 1.0, 0.0).astype(BF), wown_ref[...])
        weight = weight + dot(jnp.where(lane + 512 == idx, 1.0, 0.0).astype(BF), woth_ref[...])
        for level in range(LEVELS):
            lw_ref[at, level * D : level * D + D] = (
                weight * mix_ref[:, level : level + 1]
            ).astype(BF)


def block_kernel(
    recv_ref,
    idxr_ref,
    mix_ref,
    gain_ref,
    mcol_ref,
    mrow_ref,
    pmain_ref,
    prest_ref,
    lw_far,
    wqkv_far,
    gb_far,
    ga_far,
    tok_far,
    att_far,
    gown_far,
    goth_far,
    lw_ref,
    wqkv_ref,
    gb_ref,
    ga_ref,
    g_ref,
    a_s,
    at_s,
    t_s,
    unit_s,
    inv_s,
    norm_s,
    qkv_s,
    att_s,
    gp_s,
    bo_s,
    gt_s,
    gs_s,
    sem_in,
    sem_out,
):
    far = [lw_far, wqkv_far, gb_far, ga_far]
    near = [lw_ref, wqkv_ref, gb_ref, ga_ref]
    moves = [pltpu.make_async_copy(x, y, sem_in.at[i]) for i, (x, y) in enumerate(zip(far, near))]
    for move in moves:
        move.start()
    sent = []

    def send(source, target):
        move = pltpu.make_async_copy(source, target, sem_out.at[len(sent)])
        move.start()
        sent.append(move)

    lat = lax.axis_index("lat")
    core = lax.axis_index("core")
    gain = gain_ref[...]

    halves = []
    for half in range(2):
        src = lat if half == 0 else 1 - lat
        part = recv_ref[:, src].astype(F32)
        halves.append(part.reshape(256, LANES).astype(BF))
    for b in range(PSIDE):
        place = []
        pixels = []
        for half in range(2):
            place += [pmain_ref[half], prest_ref[half, b]]
            pixels += [halves[half][:, 256 * b : 256 * b + 256], halves[half][:, 1024:1152]]
        place = jnp.concatenate(place, axis=1)
        pixels = jnp.concatenate(pixels, axis=1)
        a_s[:, 256 * b : 256 * b + 256] = dot(place, pixels, NT).astype(BF)
        at_s[256 * b : 256 * b + 256, :] = dot(pixels, place, NT).astype(BF)
    moves[0].wait()
    for level in range(LEVELS):
        tok = dot(a_s[...], lw_ref[:, level * D : level * D + D]).astype(BF).astype(F32)
        for w in range(WINDOWS):
            t_s[w * WTOK + level * 72 : w * WTOK + level * 72 + 72, :] = tok[w * 72 : w * 72 + 72]

    bo_s[...] = t_s[...].astype(BF)
    send(bo_s, tok_far)

    def norm_step(w, carry):
        rows = pl.ds(pl.multiple_of(w * WTOK, WTOK), WTOK)
        x = t_s[rows, :]
        centred = x - jnp.mean(x, axis=-1, keepdims=True)
        inv = lax.rsqrt(jnp.mean(centred * centred, axis=-1, keepdims=True) + EPS)
        unit = centred * inv
        unit_s[rows, :] = unit
        inv_s[rows, :] = inv
        norm_s[rows, :] = (unit * gain).astype(BF)
        return carry

    lax.fori_loop(0, WINDOWS, norm_step, 0, unroll=True)
    moves[1].wait()
    for n in range(3):
        qkv_s[:, n * D : n * D + D] = dot(norm_s[...], wqkv_ref[:, n * D : n * D + D]).astype(BF)

    for move in moves[2:]:
        move.wait()
    low = lax.broadcasted_iota(jnp.int32, (1, 128), 1) < HDIM
    lane = lax.broadcasted_iota(jnp.int32, (1, 256), 1) // HDIM
    keep = [jnp.where(lane == e, 1.0, 0.0).astype(BF) for e in range(4)]

    def by_head(x):
        return jnp.concatenate([x * keep[e] for e in range(4)], axis=0)

    def own_heads(x):
        left = jnp.where(low, x[:WTOK, :128], x[WTOK : 2 * WTOK, :128])
        right = jnp.where(low, x[2 * WTOK : 3 * WTOK, 128:], x[3 * WTOK :, 128:])
        return jnp.concatenate([left, right], axis=1).astype(BF)

    def window_step(w, carry):
        rows = pl.ds(pl.multiple_of(w * WTOK, WTOK), WTOK)
        same = mcol_ref[w] == mrow_ref[w]
        state = []
        for part in range(2):
            at = part * 256
            keys = qkv_s[rows, D + at : D + at + 256]
            values = qkv_s[rows, 2 * D + at : 2 * D + at + 256]
            queries = by_head(qkv_s[rows, at : at + 256] * 0.125)
            grads = by_head(ga_ref[rows, at : at + 256])
            state.append((keys, values, queries, grads, dot(keys, queries, NT), dot(values, grads, NT)))
        ready = []
        for keys, values, queries, grads, score, gprob in state:
            score = jnp.where(same, score, -1e30)
            ex = jnp.exp(score - jnp.max(score, axis=0, keepdims=True))
            prob = ex * (1.0 / jnp.sum(ex, axis=0, keepdims=True))
            centred = gprob - jnp.sum(prob * gprob, axis=0, keepdims=True)
            ready.append(((prob * centred).astype(BF), prob.astype(BF)))
        for part in range(2):
            at = part * 256
            keys, values, queries, grads = state[part][:4]
            gscore, prob = ready[part]
            att_s[rows, at : at + 256] = own_heads(dot(prob, values, TN))
            gp_s[rows, at : at + 256] = own_heads(dot(gscore, keys * 0.125, TN))
            gp_s[rows, D + at : D + at + 256] = dot(gscore, queries).astype(BF)
            gp_s[rows, 2 * D + at : 2 * D + at + 256] = dot(prob, grads).astype(BF)
        return carry

    lax.fori_loop(0, WINDOWS, window_step, 0, unroll=4)

    send(att_s, att_far)

    total = dot(norm_s[...], gp_s[...], TN)
    for part in range(2):
        g_ref[core ^ part, :, 0:768] = total[:, 768 * part : 768 * part + 768].astype(BF)
    total = dot(att_s[...], gb_ref[...], TN)
    for part in range(2):
        g_ref[core ^ part, :, 768:1024] = total[:, 256 * part : 256 * part + 256].astype(BF)
    for i, target in enumerate((gown_far, goth_far)):
        send(g_ref.at[i, :, :1024], target.at[:, :1024])

    for part in range(2):
        rows = slice(part * PATCHES, part * PATCHES + PATCHES)
        h = dot(gp_s[rows, :], wqkv_ref[...], NT) * gain
        unit = unit_s[rows, :]
        shifted = inv_s[rows, :] * (
            h
            - jnp.mean(h, axis=-1, keepdims=True)
            - unit * jnp.mean(h * unit, axis=-1, keepdims=True)
        )
        total = (gb_ref[rows, :].astype(F32) + shifted.astype(BF).astype(F32)).astype(BF).astype(F32)
        for i in range(WINDOWS // 2):
            w = part * (WINDOWS // 2) + i
            for level in range(LEVELS):
                at = i * WTOK + level * 72
                gt_s[level, w * 72 : w * 72 + 72, :] = total[at : at + 72]

    grads = [gt_s[level].astype(BF) for level in range(LEVELS)]
    for b in range(PSIDE):
        slot = None
        for level in range(LEVELS):
            part = dot(at_s[256 * b : 256 * b + 256, :], grads[level])
            part = part * mix_ref[:, level : level + 1]
            slot = part if slot is None else slot + part
        gs_s[256 * b : 256 * b + 256, :] = slot.astype(BF)
    row = lax.broadcasted_iota(jnp.int32, (512, 1024), 0)
    idx = idxr_ref[...]
    for i, target in ((1, goth_far), (0, gown_far)):
        pick = jnp.where(row + 512 * i == idx, 1.0, 0.0).astype(BF)
        g_ref[i, :, 1024:1536] = dot(pick, gs_s[...]).astype(BF)
        send(g_ref.at[i, :, 1024:], target.at[:, 1024:])
    for move in sent:
        move.wait()


def out_kernel(tok_ref, att_ref, wproj_ref, tokt_ref, top_ref, bot_ref, side_top_ref, side_bot_ref):
    branch = dot(att_ref[...], wproj_ref[...]).astype(BF).astype(F32)
    total = (tok_ref[...].astype(F32) + branch).astype(BF)
    top_ref[...] = dot(tokt_ref[:PATCHES], total).astype(BF)
    bot_ref[...] = dot(tokt_ref[PATCHES:TOKENS], total).astype(BF)
    sides = dot(tokt_ref[TOKENS:], total).astype(BF)
    side_top_ref[...] = sides[:STRIP]
    side_bot_ref[...] = sides[STRIP : 2 * STRIP]


def add_kernel(left_ref, right_ref, out_ref):
    out_ref[...] = (left_ref[...].astype(F32) + right_ref[...].astype(F32)).astype(BF)


def join_half(part, ref, qkv_far, proj_far, qkv_s, proj_s, sems):
    moves = []
    for near, far, first in ((qkv_s, qkv_far, 0), (proj_s, proj_far, 768)):
        width = near.shape[1]
        near[...] = ref[:, first : first + width].astype(F32)
        at = pl.multiple_of((lax.axis_index("core") ^ part) * width, 256)
        move = pltpu.make_async_copy(near, far.at[:, pl.ds(at, width)], sems.at[len(moves)])
        move.start()
        moves.append(move)
    for move in moves:
        move.wait()


def own_kernel(mine_ref, *rest):
    join_half(0, mine_ref, *rest)


def other_kernel(other_ref, qkv_in, proj_in, *rest):
    join_half(1, other_ref, *rest)


def shape(*dims, dtype=BF):
    return jax.ShapeDtypeStruct(dims, dtype)


def cost(us):
    return pl.CostEstimate(flops=int(us * 1e9), bytes_accessed=0, transcendentals=0)


def vmem_call(kernel, outs, scratch=(), count=0, far=(), far_out=(), mib=58, us=1, aliases=None):
    def spec(is_far):
        return pl.BlockSpec(memory_space=pl.ANY if is_far else pltpu.VMEM)

    many = isinstance(outs, (list, tuple))
    return pl.pallas_call(
        kernel,
        out_shape=outs,
        in_specs=[spec(i in far) for i in range(count)],
        out_specs=[spec(i in far_out) for i in range(len(outs))] if many else spec(False),
        scratch_shapes=list(scratch),
        input_output_aliases=aliases or {},
        compiler_params=pltpu.CompilerParams(vmem_limit_bytes=mib * 1024 * 1024),
        cost_estimate=cost(us),
    )


def per_device(
    counts,
    pixels,
    var_order,
    embed_weight,
    level_mix,
    norm_gain,
    w_qkv,
    w_proj,
    mask_ids,
    cotangent,
):
    chips, lats, lons = counts
    bands = chips * 2
    lat = lax.axis_index("lat")
    core = lax.axis_index("core")
    lon = lax.axis_index("lon")
    rows_ring = ("chip", "core", "lat")
    everyone = ("chip", "core", "lat", "lon")
    ring = bands * lats
    group = ("chip", "lat", "lon")
    group_size = chips * lats * lons

    swap_lon = [(0, 1), (1, 0)]
    swap_core = [(0, 1), (1, 0)]

    main, edge = pixel_place()
    border, ahead, corner, copies = vmem_call(
        edge_kernel,
        [
            shape(2 * bands * 8 + 4 * STRIP, 128),
            shape(HALF, LEVELS, COLS, D),
            shape(STRIP, D),
            shape(chips, 32, D),
        ],
        count=5,
        us=3,
    )(
        pixels,
        cotangent,
        embed_weight.reshape(32, D),
        jnp.asarray(edge_place(), BF),
        jnp.asarray(strip_place(), BF),
    )
    halo = lax.ppermute(border, "lon", swap_lon)
    halo, ahead, corner = lax.optimization_barrier((halo, ahead, corner))
    ahead = lax.ppermute(ahead, rows_ring, [(i, (i - 1) % ring) for i in range(ring)])
    corner = lax.ppermute(
        corner,
        everyone,
        [(i * 2 + k, ((i - 1) % ring) * 2 + 1 - k) for i in range(ring) for k in range(2)],
    )
    own_weight = lax.all_to_all(copies, "chip", split_axis=0, concat_axis=0, tiled=True)
    own_weight = own_weight.reshape(512, D)
    oth_weight = lax.ppermute(own_weight, "core", swap_core)

    (packed,) = vmem_call(
        pack_kernel,
        [shape(bands, 2, 8, LANES)],
        [
            pltpu.VMEM((2, bands * 8, LANES), BF),
            pltpu.VMEM((LANES, LANES), BF),
            pltpu.VMEM((2, bands, 8, LANES), BF),
            pltpu.SemaphoreType.DMA((3,)),
        ],
        count=4,
        far=(3,),
        far_out=(0,),
        us=6,
    )(pixels, jnp.asarray(edge, BF), halo, jnp.asarray(main, BF))
    recv = lax.all_to_all(
        packed.reshape(bands * 2, 8, LANES), rows_ring, split_axis=0, concat_axis=0, tiled=True
    ).reshape(bands, 2, 8, LANES)

    var_order, ahead, corner = lax.optimization_barrier((var_order, ahead, corner))
    device = var_order // 2
    base = jnp.where(device % 2 == core, 0, 512) + (device // 2) * 32 + (var_order % 2) * 16
    index = base[None, :, None] + (
        jnp.arange(4)[:, None, None] + 4 * jnp.arange(4)[None, None, :]
    )
    index = index.reshape(1024).astype(jnp.int32)
    slot_mix = jnp.repeat(level_mix[var_order], 4, axis=0)

    ids = mask_ids.reshape(2, HALF, LEVELS, WINDOWS, WCOL).transpose(3, 2, 0, 1, 4)
    ids = ids.reshape(WINDOWS, WTOK)

    tok = token_place()
    level_weight, grad_branch, grad_attended = vmem_call(
        prepare_kernel, [shape(1024, 1024), shape(TOKENS, D), shape(TOKENS, D)], count=10, us=8
    )(
        index[:, None],
        slot_mix,
        own_weight,
        oth_weight,
        cotangent,
        ahead,
        halo,
        corner,
        jnp.asarray(tok, BF),
        w_proj,
    )

    pmain, prest = patch_place()
    tokens, attended, gown, goth = vmem_call(
        block_kernel,
        [
            shape(TOKENS, D),
            shape(TOKENS, D),
            shape(512, 1536),
            shape(512, 1536),
        ],
        [
            pltpu.VMEM((1024, 1024), BF),
            pltpu.VMEM((D, 3 * D), BF),
            pltpu.VMEM((TOKENS, D), BF),
            pltpu.VMEM((TOKENS, D), BF),
            pltpu.VMEM((2, 512, 1536), BF),
            pltpu.VMEM((PATCHES, 1024), BF),
            pltpu.VMEM((1024, PATCHES), BF),
            pltpu.VMEM((TOKENS, D), F32),
            pltpu.VMEM((TOKENS, D), F32),
            pltpu.VMEM((TOKENS, 1), F32),
            pltpu.VMEM((TOKENS, D), BF),
            pltpu.VMEM((TOKENS, 3 * D), BF),
            pltpu.VMEM((TOKENS, D), BF),
            pltpu.VMEM((TOKENS, 3 * D), BF),
            pltpu.VMEM((TOKENS, D), BF),
            pltpu.VMEM((LEVELS, PATCHES, D), F32),
            pltpu.VMEM((1024, D), BF),
            pltpu.SemaphoreType.DMA((4,)),
            pltpu.SemaphoreType.DMA((6,)),
        ],
        count=12,
        far=range(8, 12),
        far_out=(0, 1, 2, 3),
        us=28,
    )(
        recv,
        index[None, :],
        slot_mix,
        norm_gain[None, :],
        ids[:, :, None],
        jnp.tile(ids, (1, 4))[:, None, :],
        jnp.asarray(pmain, BF),
        jnp.asarray(prest, BF),
        level_weight,
        w_qkv,
        grad_branch,
        grad_attended,
    )

    from_core = lax.ppermute(goth, "core", swap_core)
    chip_sum = vmem_call(add_kernel, shape(512, 1536), count=2, mib=7, us=2)(gown, from_core)
    terms = lax.all_to_all(
        chip_sum.reshape(group_size, 8, 1536), group, split_axis=0, concat_axis=0, tiled=True
    )
    owned = jnp.sum(terms.astype(F32), axis=0).astype(BF)
    copies = jnp.broadcast_to(owned[None, :, :1024], (group_size, 8, 1024))
    mine = lax.all_to_all(copies, group, split_axis=0, concat_axis=0, tiled=True)
    mine = mine.reshape(512, 1024)

    embed_part = owned[:, 1024:]
    pieces = [embed_part]
    for dlat, dlon in ((0, 1), (1, 0), (1, 1)):
        pieces.append(
            lax.ppermute(
                embed_part,
                ("lat", "lon"),
                [(i * 2 + k, (i ^ dlat) * 2 + (k ^ dlon)) for i in range(2) for k in range(2)],
            )
        )
    stacked = jnp.stack(pieces)
    tile = lat * 2 + lon
    grad_embed = jnp.concatenate(
        [lax.dynamic_index_in_dim(stacked, tile ^ t, 0, keepdims=False) for t in range(4)], axis=0
    )
    grad_embed = grad_embed.reshape(2, 16, D).astype(F32)

    top, bot, side_top, side_bot = vmem_call(
        out_kernel,
        [shape(PATCHES, D), shape(PATCHES, D), shape(STRIP, D), shape(STRIP, D)],
        count=4,
        us=5,
    )(tokens, attended, w_proj, jnp.asarray(tok.T, BF))
    from_before = lax.ppermute(bot, rows_ring, [(i, (i + 1) % ring) for i in range(ring)])
    west = lax.ppermute(side_top, "lon", swap_lon)
    south_west = lax.ppermute(
        side_bot,
        everyone,
        [(i * 2 + k, ((i + 1) % ring) * 2 + 1 - k) for i in range(ring) for k in range(2)],
    )
    _, from_before, west, south_west = lax.optimization_barrier((owned, from_before, west, south_west))
    body = jnp.concatenate([from_before, top], axis=0).reshape(ROWS, LEVELS, COLS, D)
    sides = jnp.concatenate([south_west[:36], west[:36]], axis=0).reshape(ROWS, LEVELS, 3, D)
    block_out = jnp.concatenate([sides, body[:, :, 3:]], axis=2)

    mine, block_out, grad_embed = lax.optimization_barrier((mine, block_out, grad_embed))
    other = lax.ppermute(mine, "core", swap_core)
    full = [shape(512, 1536, dtype=F32), shape(512, 512, dtype=F32)]
    room = [
        pltpu.VMEM((512, 768), F32),
        pltpu.VMEM((512, 256), F32),
        pltpu.SemaphoreType.DMA((2,)),
    ]
    own = vmem_call(own_kernel, full, room, count=1, far_out=(0, 1), mib=10, us=2)(mine)
    grad_qkv, grad_proj = vmem_call(
        other_kernel, full, room, 3, (1, 2), (0, 1), mib=10, us=2, aliases={1: 0, 2: 1}
    )(other, *own)
    return (block_out, grad_embed, grad_qkv, grad_proj)


def solution(mesh):
    var, lats, lons = (mesh.shape[name] for name in ("var", "lat", "lon"))
    chips = var // 2
    fine = Mesh(mesh.devices.reshape(chips, 2, lats, lons), ("chip", "core", "lat", "lon"))
    both = ("chip", "core")
    in_specs = (
        P(None, "lat", both, None, "lon"),
        P(),
        P(both, None, None),
        P(),
        P(),
        P(),
        P(),
        P(("chip", "core", "lat"), None, "lon"),
        P(("chip", "core", "lat"), None, "lon", None),
    )
    out_specs = (P(("chip", "core", "lat"), None, "lon", None), P(both, None, None), P(), P())
    return jax.shard_map(
        functools.partial(per_device, (chips, lats, lons)),
        mesh=fine,
        in_specs=in_specs,
        out_specs=out_specs,
        check_vma=False,
    )
```

```python
import functools

import jax
import jax.numpy as jnp
import numpy as np
from jax import lax
from jax.experimental import pallas as pl
from jax.experimental.pallas import tpu as pltpu
from jax.sharding import Mesh, PartitionSpec as P

D = 512
HEADS = 8
HDIM = 64
PSIDE = 4
WCOL = 6
ROWS = 12
HALF = 6
COLS = 48
WINDOWS = 8
LEVELS = 2
TOKENS = 1152
WTOK = 144
PATCHES = 576
LANES = 1152
STRIP = 48
EPS = 1e-05
BF = jnp.bfloat16
F32 = jnp.float32

NN = (((1,), (0,)), ((), ()))
NT = (((1,), (1,)), ((), ()))
TN = (((0,), (0,)), ((), ()))


def dot(a, b, dims=NN):
    return lax.dot_general(a, b, dims, preferred_element_type=F32)


def patch_index(w, j, c6):
    if w == WINDOWS - 1:
        return 252 + j * 3 + c6 if c6 < 3 else 267 + j * 3 + c6
    return w * 36 + j * WCOL + c6


def pixel_lane(b, patch):
    return 256 * b + patch if patch < 256 else 1024 + 32 * b + patch - 256


def edge_place():
    place = np.zeros((HALF, 128, 128), np.float32)
    for j in range(HALF):
        lane = np.arange(12)
        place[j, lane, j * 12 + lane] = 1
    return place


def pixel_place():
    main = np.zeros((HALF * PSIDE * COLS, LANES), np.float32)
    edge = np.zeros((128, 128), np.float32)
    for j in range(HALF):
        for c in range(COLS):
            for b in range(PSIDE):
                col = c - 3 if c >= 3 else COLS - 3 + c
                lane = pixel_lane(b, patch_index(col // WCOL, j, col % WCOL))
                if c >= 3:
                    main[(j * COLS + c) * PSIDE + b, lane] = 1
                else:
                    edge[j * 12 + c * PSIDE + b, lane - 1024] = 1
    return main, edge


def patch_place():
    main = np.zeros((2, PATCHES, 256), np.float32)
    rest = np.zeros((2, PSIDE, PATCHES, 128), np.float32)
    for half in range(2):
        for w in range(WINDOWS):
            for i in range(36):
                patch = patch_index(w, i // WCOL, i % WCOL)
                row = w * 72 + half * 36 + i
                if patch < 256:
                    main[half, row, patch] = 1
                else:
                    for b in range(PSIDE):
                        rest[half, b, row, 32 * b + patch - 256] = 1
    return main, rest


def token_place():
    place = np.zeros((TOKENS, TOKENS + 128), np.float32)
    for w in range(WINDOWS):
        for level in range(LEVELS):
            for half in range(2):
                for j in range(HALF):
                    for c6 in range(WCOL):
                        t = w * WTOK + level * 72 + half * 36 + j * WCOL + c6
                        c = w * WCOL + c6 + 3
                        if c < COLS:
                            place[t, half * PATCHES + (j * LEVELS + level) * COLS + c] = 1
                        else:
                            place[t, TOKENS + half * STRIP + (j * LEVELS + level) * 3 + c - COLS] = 1
    return place


def half_rows(pix_ref, half, j, lanes):
    rows = pix_ref[:, half * HALF + j, :, :, :lanes].astype(F32)
    merged = jnp.concatenate([rows[:, 0], rows[:, 1]], axis=1)
    return merged.reshape(merged.shape[0] * 8, lanes)


def strip_place():
    place = np.zeros((2 * STRIP, ROWS * LEVELS * 16), np.float32)
    for half in range(2):
        for i in range(HALF * LEVELS):
            for c in range(3):
                place[half * STRIP + i * 3 + c, (half * HALF * LEVELS + i) * 16 + c] = 1
    return place


def edge_kernel(
    pix_ref, cot_ref, weight_ref, place_ref, strip_ref, west_ref, ahead_ref, corner_ref, copies_ref
):
    size = (west_ref.shape[0] - 4 * STRIP) // 2
    for half in range(2):
        total = None
        for j in range(HALF):
            term = dot(half_rows(pix_ref, half, j, 128).astype(BF), place_ref[j])
            total = term if total is None else total + term
        west_ref[half * size : half * size + size, :] = total.astype(BF)
    strips = cot_ref[:, :, :16, :].reshape(ROWS * LEVELS * 16, D)
    strips = dot(strip_ref[...], strips).astype(BF)
    corner_ref[...] = strips[:STRIP]
    for t in range(4):
        at = 2 * size + t * STRIP
        west_ref[at : at + STRIP, :] = strips[STRIP:, 128 * t : 128 * t + 128]
    ahead_ref[...] = cot_ref[:HALF]
    copies_ref[...] = jnp.broadcast_to(weight_ref[...][None], copies_ref.shape)


def pack_kernel(pix_ref, edge_ref, halo_ref, main_ref, out_ref, rows_s, main_s, out_s, sems):
    move = pltpu.make_async_copy(main_ref, main_s, sems.at[0])
    move.start()
    lat = lax.axis_index("lat")
    bands = out_ref.shape[0]
    size = bands * 8
    moves = []
    for half in range(2):
        for i in range(HALF // 2):
            pair = [half_rows(pix_ref, half, 2 * i + k, 4 * COLS) for k in range(2)]
            rows_s[half, :, 384 * i : 384 * i + 384] = jnp.concatenate(pair, axis=1).astype(BF)
        if half == 0:
            move.wait()
        for n in range(3):
            lanes = slice(384 * n, 384 * n + 384)
            block = dot(rows_s[half], main_s[:, lanes])
            if n == 2:
                halo = dot(halo_ref[half * size : half * size + size, :], edge_ref[...])
                block = jnp.concatenate([block[:, :256], block[:, 256:] + halo], axis=1)
            block = block.reshape(bands, 8, 384)
            if half == 0:
                later = jnp.concatenate([block[1:], block[:1]], axis=0)
                block = jnp.where(lat == 0, later, block)
            out_s[half, :, :, lanes] = block.astype(BF)
        target = lat if half == 1 else 1 - lat
        moves.append(pltpu.make_async_copy(out_s.at[half], out_ref.at[:, target], sems.at[1 + half]))
        moves[half].start()
    for move in moves:
        move.wait()


def prepare_kernel(
    idx_ref,
    mix_ref,
    wown_ref,
    woth_ref,
    cot_ref,
    ahead_ref,
    halo_ref,
    corner_ref,
    tok_ref,
    wproj_ref,
    lw_ref,
    gb_ref,
    ga_ref,
):
    start = halo_ref.shape[0] - 4 * STRIP
    east = jnp.concatenate(
        [halo_ref[start + STRIP * t : start + STRIP * t + STRIP, :] for t in range(4)], axis=1
    )
    sides = jnp.concatenate([east, corner_ref[...], jnp.zeros((128 - 2 * STRIP, D), BF)], axis=0)
    gb = dot(tok_ref[:, :PATCHES], cot_ref[HALF:].reshape(PATCHES, D))
    gb = gb + dot(tok_ref[:, PATCHES:TOKENS], ahead_ref[...].reshape(PATCHES, D))
    gb = gb + dot(tok_ref[:, TOKENS:], sides)
    gb_ref[...] = gb.astype(BF)
    ga_ref[...] = dot(gb_ref[...], wproj_ref[...], NT).astype(BF)
    lane = lax.broadcasted_iota(jnp.int32, (256, 512), 1)
    for b in range(PSIDE):
        at = slice(256 * b, 256 * b + 256)
        idx = idx_ref[at, :]
        weight = dot(jnp.where(lane == idx, 1.0, 0.0).astype(BF), wown_ref[...])
        weight = weight + dot(jnp.where(lane + 512 == idx, 1.0, 0.0).astype(BF), woth_ref[...])
        for level in range(LEVELS):
            lw_ref[at, level * D : level * D + D] = (
                weight * mix_ref[:, level : level + 1]
            ).astype(BF)


def block_kernel(
    recv_ref,
    idxr_ref,
    mix_ref,
    gain_ref,
    mcol_ref,
    mrow_ref,
    pmain_ref,
    prest_ref,
    lw_far,
    wqkv_far,
    gb_far,
    ga_far,
    tok_far,
    att_far,
    gown_far,
    goth_far,
    lw_ref,
    wqkv_ref,
    gb_ref,
    ga_ref,
    g_ref,
    a_s,
    at_s,
    t_s,
    unit_s,
    inv_s,
    norm_s,
    qkv_s,
    att_s,
    gp_s,
    bo_s,
    gt_s,
    gs_s,
    sem_in,
    sem_out,
):
    far = [lw_far, wqkv_far, gb_far, ga_far]
    near = [lw_ref, wqkv_ref, gb_ref, ga_ref]
    moves = [pltpu.make_async_copy(x, y, sem_in.at[i]) for i, (x, y) in enumerate(zip(far, near))]
    for move in moves:
        move.start()
    sent = []

    def send(source, target):
        move = pltpu.make_async_copy(source, target, sem_out.at[len(sent)])
        move.start()
        sent.append(move)

    lat = lax.axis_index("lat")
    core = lax.axis_index("core")
    gain = gain_ref[...]

    halves = []
    for half in range(2):
        src = lat if half == 0 else 1 - lat
        part = recv_ref[:, src].astype(F32)
        halves.append(part.reshape(256, LANES).astype(BF))
    for b in range(PSIDE):
        place = []
        pixels = []
        for half in range(2):
            place += [pmain_ref[half], prest_ref[half, b]]
            pixels += [halves[half][:, 256 * b : 256 * b + 256], halves[half][:, 1024:1152]]
        place = jnp.concatenate(place, axis=1)
        pixels = jnp.concatenate(pixels, axis=1)
        a_s[:, 256 * b : 256 * b + 256] = dot(place, pixels, NT).astype(BF)
        at_s[256 * b : 256 * b + 256, :] = dot(pixels, place, NT).astype(BF)
    moves[0].wait()
    for level in range(LEVELS):
        tok = dot(a_s[...], lw_ref[:, level * D : level * D + D]).astype(BF).astype(F32)
        for w in range(WINDOWS):
            t_s[w * WTOK + level * 72 : w * WTOK + level * 72 + 72, :] = tok[w * 72 : w * 72 + 72]

    bo_s[...] = t_s[...].astype(BF)
    send(bo_s, tok_far)

    def norm_step(w, carry):
        rows = pl.ds(pl.multiple_of(w * WTOK, WTOK), WTOK)
        x = t_s[rows, :]
        centred = x - jnp.mean(x, axis=-1, keepdims=True)
        inv = lax.rsqrt(jnp.mean(centred * centred, axis=-1, keepdims=True) + EPS)
        unit = centred * inv
        unit_s[rows, :] = unit
        inv_s[rows, :] = inv
        norm_s[rows, :] = (unit * gain).astype(BF)
        return carry

    lax.fori_loop(0, WINDOWS, norm_step, 0, unroll=True)
    moves[1].wait()
    for n in range(3):
        qkv_s[:, n * D : n * D + D] = dot(norm_s[...], wqkv_ref[:, n * D : n * D + D]).astype(BF)

    for move in moves[2:]:
        move.wait()
    low = lax.broadcasted_iota(jnp.int32, (1, 128), 1) < HDIM
    lane = lax.broadcasted_iota(jnp.int32, (1, 256), 1) // HDIM
    keep = [jnp.where(lane == e, 1.0, 0.0).astype(BF) for e in range(4)]

    def by_head(x):
        return jnp.concatenate([x * keep[e] for e in range(4)], axis=0)

    def own_heads(x):
        left = jnp.where(low, x[:WTOK, :128], x[WTOK : 2 * WTOK, :128])
        right = jnp.where(low, x[2 * WTOK : 3 * WTOK, 128:], x[3 * WTOK :, 128:])
        return jnp.concatenate([left, right], axis=1).astype(BF)

    def window_step(w, carry):
        rows = pl.ds(pl.multiple_of(w * WTOK, WTOK), WTOK)
        same = mcol_ref[w] == mrow_ref[w]
        state = []
        for part in range(2):
            at = part * 256
            keys = qkv_s[rows, D + at : D + at + 256]
            values = qkv_s[rows, 2 * D + at : 2 * D + at + 256]
            queries = by_head(qkv_s[rows, at : at + 256] * 0.125)
            grads = by_head(ga_ref[rows, at : at + 256])
            state.append((keys, values, queries, grads, dot(keys, queries, NT), dot(values, grads, NT)))
        ready = []
        for keys, values, queries, grads, score, gprob in state:
            score = jnp.where(same, score, -1e30)
            ex = jnp.exp(score - jnp.max(score, axis=0, keepdims=True))
            prob = ex * (1.0 / jnp.sum(ex, axis=0, keepdims=True))
            centred = gprob - jnp.sum(prob * gprob, axis=0, keepdims=True)
            ready.append(((prob * centred).astype(BF), prob.astype(BF)))
        for part in range(2):
            at = part * 256
            keys, values, queries, grads = state[part][:4]
            gscore, prob = ready[part]
            att_s[rows, at : at + 256] = own_heads(dot(prob, values, TN))
            gp_s[rows, at : at + 256] = own_heads(dot(gscore, keys * 0.125, TN))
            gp_s[rows, D + at : D + at + 256] = dot(gscore, queries).astype(BF)
            gp_s[rows, 2 * D + at : 2 * D + at + 256] = dot(prob, grads).astype(BF)
        return carry

    lax.fori_loop(0, WINDOWS, window_step, 0, unroll=4)

    send(att_s, att_far)

    total = dot(norm_s[...], gp_s[...], TN)
    for part in range(2):
        g_ref[core ^ part, :, 0:768] = total[:, 768 * part : 768 * part + 768].astype(BF)
    total = dot(att_s[...], gb_ref[...], TN)
    for part in range(2):
        g_ref[core ^ part, :, 768:1024] = total[:, 256 * part : 256 * part + 256].astype(BF)
    for i, target in enumerate((gown_far, goth_far)):
        send(g_ref.at[i, :, :1024], target.at[:, :1024])

    for part in range(2):
        rows = slice(part * PATCHES, part * PATCHES + PATCHES)
        h = dot(gp_s[rows, :], wqkv_ref[...], NT) * gain
        unit = unit_s[rows, :]
        shifted = inv_s[rows, :] * (
            h
            - jnp.mean(h, axis=-1, keepdims=True)
            - unit * jnp.mean(h * unit, axis=-1, keepdims=True)
        )
        total = (gb_ref[rows, :].astype(F32) + shifted.astype(BF).astype(F32)).astype(BF).astype(F32)
        for i in range(WINDOWS // 2):
            w = part * (WINDOWS // 2) + i
            for level in range(LEVELS):
                at = i * WTOK + level * 72
                gt_s[level, w * 72 : w * 72 + 72, :] = total[at : at + 72]

    grads = [gt_s[level].astype(BF) for level in range(LEVELS)]
    for b in range(PSIDE):
        slot = None
        for level in range(LEVELS):
            part = dot(at_s[256 * b : 256 * b + 256, :], grads[level])
            part = part * mix_ref[:, level : level + 1]
            slot = part if slot is None else slot + part
        gs_s[256 * b : 256 * b + 256, :] = slot.astype(BF)
    row = lax.broadcasted_iota(jnp.int32, (512, 1024), 0)
    idx = idxr_ref[...]
    for i, target in ((1, goth_far), (0, gown_far)):
        pick = jnp.where(row + 512 * i == idx, 1.0, 0.0).astype(BF)
        g_ref[i, :, 1024:1536] = dot(pick, gs_s[...]).astype(BF)
        send(g_ref.at[i, :, 1024:], target.at[:, 1024:])
    for move in sent:
        move.wait()


def out_kernel(tok_ref, att_ref, wproj_ref, tokt_ref, top_ref, bot_ref, side_top_ref, side_bot_ref):
    branch = dot(att_ref[...], wproj_ref[...]).astype(BF).astype(F32)
    total = (tok_ref[...].astype(F32) + branch).astype(BF)
    top_ref[...] = dot(tokt_ref[:PATCHES], total).astype(BF)
    bot_ref[...] = dot(tokt_ref[PATCHES:TOKENS], total).astype(BF)
    sides = dot(tokt_ref[TOKENS:], total).astype(BF)
    side_top_ref[...] = sides[:STRIP]
    side_bot_ref[...] = sides[STRIP : 2 * STRIP]


def add_kernel(left_ref, right_ref, out_ref):
    out_ref[...] = (left_ref[...] + right_ref[...].astype(F32)).astype(BF)


def join_half(part, ref, qkv_far, proj_far, qkv_s, proj_s, sems):
    moves = []
    for near, far, first in ((qkv_s, qkv_far, 0), (proj_s, proj_far, 768)):
        width = near.shape[1]
        near[...] = ref[:, first : first + width].astype(F32)
        at = pl.multiple_of((lax.axis_index("core") ^ part) * width, 256)
        move = pltpu.make_async_copy(near, far.at[:, pl.ds(at, width)], sems.at[len(moves)])
        move.start()
        moves.append(move)
    for move in moves:
        move.wait()


def own_kernel(mine_ref, *rest):
    join_half(0, mine_ref, *rest)


def other_kernel(other_ref, qkv_in, proj_in, *rest):
    join_half(1, other_ref, *rest)


def shape(*dims, dtype=BF):
    return jax.ShapeDtypeStruct(dims, dtype)


def cost(us):
    return pl.CostEstimate(flops=int(us * 1e9), bytes_accessed=0, transcendentals=0)


def vmem_call(kernel, outs, scratch=(), count=0, far=(), far_out=(), mib=58, us=1, aliases=None):
    def spec(is_far):
        return pl.BlockSpec(memory_space=pl.ANY if is_far else pltpu.VMEM)

    many = isinstance(outs, (list, tuple))
    return pl.pallas_call(
        kernel,
        out_shape=outs,
        in_specs=[spec(i in far) for i in range(count)],
        out_specs=[spec(i in far_out) for i in range(len(outs))] if many else spec(False),
        scratch_shapes=list(scratch),
        input_output_aliases=aliases or {},
        compiler_params=pltpu.CompilerParams(vmem_limit_bytes=mib * 1024 * 1024),
        cost_estimate=cost(us),
    )


def per_device(
    counts,
    pixels,
    var_order,
    embed_weight,
    level_mix,
    norm_gain,
    w_qkv,
    w_proj,
    mask_ids,
    cotangent,
):
    chips, lats, lons = counts
    bands = chips * 2
    lat = lax.axis_index("lat")
    core = lax.axis_index("core")
    lon = lax.axis_index("lon")
    rows_ring = ("chip", "core", "lat")
    everyone = ("chip", "core", "lat", "lon")
    ring = bands * lats
    group = ("chip", "lat", "lon")
    group_size = chips * lats * lons

    swap_lon = [(0, 1), (1, 0)]
    swap_core = [(0, 1), (1, 0)]

    main, edge = pixel_place()
    border, ahead, corner, copies = vmem_call(
        edge_kernel,
        [
            shape(2 * bands * 8 + 4 * STRIP, 128),
            shape(HALF, LEVELS, COLS, D),
            shape(STRIP, D),
            shape(chips, 32, D),
        ],
        count=5,
        us=3,
    )(
        pixels,
        cotangent,
        embed_weight.reshape(32, D),
        jnp.asarray(edge_place(), BF),
        jnp.asarray(strip_place(), BF),
    )
    halo = lax.ppermute(border, "lon", swap_lon)
    halo, ahead, corner = lax.optimization_barrier((halo, ahead, corner))
    ahead = lax.ppermute(ahead, rows_ring, [(i, (i - 1) % ring) for i in range(ring)])
    corner = lax.ppermute(
        corner,
        everyone,
        [(i * 2 + k, ((i - 1) % ring) * 2 + 1 - k) for i in range(ring) for k in range(2)],
    )
    own_weight = lax.all_to_all(copies, "chip", split_axis=0, concat_axis=0, tiled=True)
    own_weight = own_weight.reshape(512, D)
    oth_weight = lax.ppermute(own_weight, "core", swap_core)

    (packed,) = vmem_call(
        pack_kernel,
        [shape(bands, 2, 8, LANES)],
        [
            pltpu.VMEM((2, bands * 8, LANES), BF),
            pltpu.VMEM((LANES, LANES), BF),
            pltpu.VMEM((2, bands, 8, LANES), BF),
            pltpu.SemaphoreType.DMA((3,)),
        ],
        count=4,
        far=(3,),
        far_out=(0,),
        us=6,
    )(pixels, jnp.asarray(edge, BF), halo, jnp.asarray(main, BF))
    recv = lax.all_to_all(
        packed.reshape(bands * 2, 8, LANES), rows_ring, split_axis=0, concat_axis=0, tiled=True
    ).reshape(bands, 2, 8, LANES)

    var_order, ahead, corner = lax.optimization_barrier((var_order, ahead, corner))
    device = var_order // 2
    base = jnp.where(device % 2 == core, 0, 512) + (device // 2) * 32 + (var_order % 2) * 16
    index = base[None, :, None] + (
        jnp.arange(4)[:, None, None] + 4 * jnp.arange(4)[None, None, :]
    )
    index = index.reshape(1024).astype(jnp.int32)
    slot_mix = jnp.repeat(level_mix[var_order], 4, axis=0)

    ids = mask_ids.reshape(2, HALF, LEVELS, WINDOWS, WCOL).transpose(3, 2, 0, 1, 4)
    ids = ids.reshape(WINDOWS, WTOK)

    tok = token_place()
    level_weight, grad_branch, grad_attended = vmem_call(
        prepare_kernel, [shape(1024, 1024), shape(TOKENS, D), shape(TOKENS, D)], count=10, us=8
    )(
        index[:, None],
        slot_mix,
        own_weight,
        oth_weight,
        cotangent,
        ahead,
        halo,
        corner,
        jnp.asarray(tok, BF),
        w_proj,
    )

    pmain, prest = patch_place()
    tokens, attended, gown, goth = vmem_call(
        block_kernel,
        [
            shape(TOKENS, D),
            shape(TOKENS, D),
            shape(512, 1536),
            shape(512, 1536),
        ],
        [
            pltpu.VMEM((1024, 1024), BF),
            pltpu.VMEM((D, 3 * D), BF),
            pltpu.VMEM((TOKENS, D), BF),
            pltpu.VMEM((TOKENS, D), BF),
            pltpu.VMEM((2, 512, 1536), BF),
            pltpu.VMEM((PATCHES, 1024), BF),
            pltpu.VMEM((1024, PATCHES), BF),
            pltpu.VMEM((TOKENS, D), F32),
            pltpu.VMEM((TOKENS, D), F32),
            pltpu.VMEM((TOKENS, 1), F32),
            pltpu.VMEM((TOKENS, D), BF),
            pltpu.VMEM((TOKENS, 3 * D), BF),
            pltpu.VMEM((TOKENS, D), BF),
            pltpu.VMEM((TOKENS, 3 * D), BF),
            pltpu.VMEM((TOKENS, D), BF),
            pltpu.VMEM((LEVELS, PATCHES, D), F32),
            pltpu.VMEM((1024, D), BF),
            pltpu.SemaphoreType.DMA((4,)),
            pltpu.SemaphoreType.DMA((6,)),
        ],
        count=12,
        far=range(8, 12),
        far_out=(0, 1, 2, 3),
        us=28,
    )(
        recv,
        index[None, :],
        slot_mix,
        norm_gain[None, :],
        ids[:, :, None],
        jnp.tile(ids, (1, 4))[:, None, :],
        jnp.asarray(pmain, BF),
        jnp.asarray(prest, BF),
        level_weight,
        w_qkv,
        grad_branch,
        grad_attended,
    )

    from_core = lax.ppermute(goth, "core", swap_core)
    wide = gown.astype(F32)
    chip_sum = vmem_call(add_kernel, shape(512, 1536), count=2, mib=12, us=2)(wide, from_core)
    terms = lax.all_to_all(
        chip_sum.reshape(group_size, 8, 1536), group, split_axis=0, concat_axis=0, tiled=True
    )
    owned = jnp.sum(terms.astype(F32), axis=0).astype(BF)
    copies = jnp.broadcast_to(owned[None, :, :1024], (group_size, 8, 1024))
    mine = lax.all_to_all(copies, group, split_axis=0, concat_axis=0, tiled=True)
    mine = mine.reshape(512, 1024)

    embed_part = owned[:, 1024:]
    pieces = [embed_part]
    for dlat, dlon in ((0, 1), (1, 0), (1, 1)):
        pieces.append(
            lax.ppermute(
                embed_part,
                ("lat", "lon"),
                [(i * 2 + k, (i ^ dlat) * 2 + (k ^ dlon)) for i in range(2) for k in range(2)],
            )
        )
    stacked = jnp.stack(pieces)
    tile = lat * 2 + lon
    grad_embed = jnp.concatenate(
        [lax.dynamic_index_in_dim(stacked, tile ^ t, 0, keepdims=False) for t in range(4)], axis=0
    )
    grad_embed = grad_embed.reshape(2, 16, D).astype(F32)

    top, bot, side_top, side_bot = vmem_call(
        out_kernel,
        [shape(PATCHES, D), shape(PATCHES, D), shape(STRIP, D), shape(STRIP, D)],
        count=4,
        us=5,
    )(tokens, attended, w_proj, jnp.asarray(tok.T, BF))
    from_before = lax.ppermute(bot, rows_ring, [(i, (i + 1) % ring) for i in range(ring)])
    west = lax.ppermute(side_top, "lon", swap_lon)
    south_west = lax.ppermute(
        side_bot,
        everyone,
        [(i * 2 + k, ((i + 1) % ring) * 2 + 1 - k) for i in range(ring) for k in range(2)],
    )
    _, from_before, west, south_west = lax.optimization_barrier((owned, from_before, west, south_west))
    body = jnp.concatenate([from_before, top], axis=0).reshape(ROWS, LEVELS, COLS, D)
    sides = jnp.concatenate([south_west[:36], west[:36]], axis=0).reshape(ROWS, LEVELS, 3, D)
    block_out = jnp.concatenate([sides, body[:, :, 3:]], axis=2)

    mine, block_out, grad_embed = lax.optimization_barrier((mine, block_out, grad_embed))
    other = lax.ppermute(mine, "core", swap_core)
    full = [shape(512, 1536, dtype=F32), shape(512, 512, dtype=F32)]
    room = [
        pltpu.VMEM((512, 768), F32),
        pltpu.VMEM((512, 256), F32),
        pltpu.SemaphoreType.DMA((2,)),
    ]
    own = vmem_call(own_kernel, full, room, count=1, far_out=(0, 1), mib=10, us=2)(mine)
    grad_qkv, grad_proj = vmem_call(
        other_kernel, full, room, 3, (1, 2), (0, 1), mib=10, us=2, aliases={1: 0, 2: 1}
    )(other, *own)
    return (block_out, grad_embed, grad_qkv, grad_proj)


def solution(mesh):
    var, lats, lons = (mesh.shape[name] for name in ("var", "lat", "lon"))
    chips = var // 2
    fine = Mesh(mesh.devices.reshape(chips, 2, lats, lons), ("chip", "core", "lat", "lon"))
    both = ("chip", "core")
    in_specs = (
        P(None, "lat", both, None, "lon"),
        P(),
        P(both, None, None),
        P(),
        P(),
        P(),
        P(),
        P(("chip", "core", "lat"), None, "lon"),
        P(("chip", "core", "lat"), None, "lon", None),
    )
    out_specs = (P(("chip", "core", "lat"), None, "lon", None), P(both, None, None), P(), P())
    return jax.shard_map(
        functools.partial(per_device, (chips, lats, lons)),
        mesh=fine,
        in_specs=in_specs,
        out_specs=out_specs,
        check_vma=False,
    )
```

```python
import functools

import jax
import jax.numpy as jnp
import numpy as np
from jax import lax
from jax.experimental import pallas as pl
from jax.experimental.pallas import tpu as pltpu
from jax.sharding import Mesh, PartitionSpec as P

D = 512
HEADS = 8
HDIM = 64
PSIDE = 4
WCOL = 6
ROWS = 12
HALF = 6
COLS = 48
WINDOWS = 8
LEVELS = 2
TOKENS = 1152
WTOK = 144
PATCHES = 576
LANES = 1152
STRIP = 48
EPS = 1e-05
BF = jnp.bfloat16
F32 = jnp.float32

NN = (((1,), (0,)), ((), ()))
NT = (((1,), (1,)), ((), ()))
TN = (((0,), (0,)), ((), ()))


def dot(a, b, dims=NN):
    return lax.dot_general(a, b, dims, preferred_element_type=F32)


def patch_index(w, j, c6):
    if w == WINDOWS - 1:
        return 252 + j * 3 + c6 if c6 < 3 else 267 + j * 3 + c6
    return w * 36 + j * WCOL + c6


def pixel_lane(b, patch):
    return 256 * b + patch if patch < 256 else 1024 + 32 * b + patch - 256


def edge_place():
    place = np.zeros((HALF, 128, 128), np.float32)
    for j in range(HALF):
        lane = np.arange(12)
        place[j, lane, j * 12 + lane] = 1
    return place


def pixel_place():
    main = np.zeros((HALF * PSIDE * COLS, LANES), np.float32)
    edge = np.zeros((128, 128), np.float32)
    for j in range(HALF):
        for c in range(COLS):
            for b in range(PSIDE):
                col = c - 3 if c >= 3 else COLS - 3 + c
                lane = pixel_lane(b, patch_index(col // WCOL, j, col % WCOL))
                if c >= 3:
                    main[(j * COLS + c) * PSIDE + b, lane] = 1
                else:
                    edge[j * 12 + c * PSIDE + b, lane - 1024] = 1
    return main, edge


def patch_place():
    main = np.zeros((2, PATCHES, 256), np.float32)
    rest = np.zeros((2, PSIDE, PATCHES, 128), np.float32)
    for half in range(2):
        for w in range(WINDOWS):
            for i in range(36):
                patch = patch_index(w, i // WCOL, i % WCOL)
                row = w * 72 + half * 36 + i
                if patch < 256:
                    main[half, row, patch] = 1
                else:
                    for b in range(PSIDE):
                        rest[half, b, row, 32 * b + patch - 256] = 1
    return main, rest


def token_place():
    place = np.zeros((TOKENS, TOKENS + 128), np.float32)
    for w in range(WINDOWS):
        for level in range(LEVELS):
            for half in range(2):
                for j in range(HALF):
                    for c6 in range(WCOL):
                        t = w * WTOK + level * 72 + half * 36 + j * WCOL + c6
                        c = w * WCOL + c6 + 3
                        if c < COLS:
                            place[t, half * PATCHES + (j * LEVELS + level) * COLS + c] = 1
                        else:
                            place[t, TOKENS + half * STRIP + (j * LEVELS + level) * 3 + c - COLS] = 1
    return place


def half_rows(pix_ref, half, j, lanes):
    rows = pix_ref[:, half * HALF + j, :, :, :lanes].astype(F32)
    merged = jnp.concatenate([rows[:, 0], rows[:, 1]], axis=1)
    return merged.reshape(merged.shape[0] * 8, lanes)


def strip_place():
    place = np.zeros((2 * STRIP, ROWS * LEVELS * 16), np.float32)
    for half in range(2):
        for i in range(HALF * LEVELS):
            for c in range(3):
                place[half * STRIP + i * 3 + c, (half * HALF * LEVELS + i) * 16 + c] = 1
    return place


def edge_kernel(
    pix_ref, cot_ref, weight_ref, place_ref, strip_ref, west_ref, ahead_ref, corner_ref, copies_ref
):
    size = (west_ref.shape[0] - 4 * STRIP) // 2
    for half in range(2):
        total = None
        for j in range(HALF):
            term = dot(half_rows(pix_ref, half, j, 128).astype(BF), place_ref[j])
            total = term if total is None else total + term
        west_ref[half * size : half * size + size, :] = total.astype(BF)
    strips = cot_ref[:, :, :16, :].reshape(ROWS * LEVELS * 16, D)
    strips = dot(strip_ref[...], strips).astype(BF)
    corner_ref[...] = strips[:STRIP]
    for t in range(4):
        at = 2 * size + t * STRIP
        west_ref[at : at + STRIP, :] = strips[STRIP:, 128 * t : 128 * t + 128]
    ahead_ref[...] = cot_ref[:HALF]
    copies_ref[...] = jnp.broadcast_to(weight_ref[...][None], copies_ref.shape)


def pack_kernel(pix_ref, edge_ref, halo_ref, main_ref, out_ref, rows_s, main_s, out_s, sems):
    move = pltpu.make_async_copy(main_ref, main_s, sems.at[0])
    move.start()
    lat = lax.axis_index("lat")
    bands = out_ref.shape[0]
    size = bands * 8
    moves = []
    for half in range(2):
        for i in range(HALF // 2):
            pair = [half_rows(pix_ref, half, 2 * i + k, 4 * COLS) for k in range(2)]
            rows_s[half, :, 384 * i : 384 * i + 384] = jnp.concatenate(pair, axis=1).astype(BF)
        if half == 0:
            move.wait()
        for n in range(3):
            lanes = slice(384 * n, 384 * n + 384)
            block = dot(rows_s[half], main_s[:, lanes])
            if n == 2:
                halo = dot(halo_ref[half * size : half * size + size, :], edge_ref[...])
                block = jnp.concatenate([block[:, :256], block[:, 256:] + halo], axis=1)
            block = block.reshape(bands, 8, 384)
            if half == 0:
                later = jnp.concatenate([block[1:], block[:1]], axis=0)
                block = jnp.where(lat == 0, later, block)
            out_s[half, :, :, lanes] = block.astype(BF)
        target = lat if half == 1 else 1 - lat
        moves.append(pltpu.make_async_copy(out_s.at[half], out_ref.at[:, target], sems.at[1 + half]))
        moves[half].start()
    for move in moves:
        move.wait()


def prepare_kernel(
    idx_ref,
    mix_ref,
    wown_ref,
    woth_ref,
    cot_ref,
    ahead_ref,
    halo_ref,
    corner_ref,
    tok_ref,
    wproj_ref,
    lw_ref,
    gb_ref,
    ga_ref,
):
    start = halo_ref.shape[0] - 4 * STRIP
    east = jnp.concatenate(
        [halo_ref[start + STRIP * t : start + STRIP * t + STRIP, :] for t in range(4)], axis=1
    )
    sides = jnp.concatenate([east, corner_ref[...], jnp.zeros((128 - 2 * STRIP, D), BF)], axis=0)
    gb = dot(tok_ref[:, :PATCHES], cot_ref[HALF:].reshape(PATCHES, D))
    gb = gb + dot(tok_ref[:, PATCHES:TOKENS], ahead_ref[...].reshape(PATCHES, D))
    gb = gb + dot(tok_ref[:, TOKENS:], sides)
    gb_ref[...] = gb.astype(BF)
    ga_ref[...] = dot(gb_ref[...], wproj_ref[...], NT).astype(BF)
    lane = lax.broadcasted_iota(jnp.int32, (256, 512), 1)
    for b in range(PSIDE):
        at = slice(256 * b, 256 * b + 256)
        idx = idx_ref[at, :]
        weight = dot(jnp.where(lane == idx, 1.0, 0.0).astype(BF), wown_ref[...])
        weight = weight + dot(jnp.where(lane + 512 == idx, 1.0, 0.0).astype(BF), woth_ref[...])
        for level in range(LEVELS):
            lw_ref[at, level * D : level * D + D] = (
                weight * mix_ref[:, level : level + 1]
            ).astype(BF)


def block_kernel(
    recv_ref,
    idxr_ref,
    mix_ref,
    gain_ref,
    mcol_ref,
    mrow_ref,
    pmain_ref,
    prest_ref,
    lw_far,
    wqkv_far,
    gb_far,
    ga_far,
    tok_far,
    att_far,
    gown_far,
    goth_far,
    lw_ref,
    wqkv_ref,
    gb_ref,
    ga_ref,
    g_ref,
    a_s,
    at_s,
    t_s,
    unit_s,
    inv_s,
    norm_s,
    qkv_s,
    att_s,
    gp_s,
    bo_s,
    gt_s,
    gs_s,
    sem_in,
    sem_out,
):
    far = [lw_far, wqkv_far, gb_far, ga_far]
    near = [lw_ref, wqkv_ref, gb_ref, ga_ref]
    moves = [pltpu.make_async_copy(x, y, sem_in.at[i]) for i, (x, y) in enumerate(zip(far, near))]
    for move in moves:
        move.start()
    sent = []

    def send(source, target):
        move = pltpu.make_async_copy(source, target, sem_out.at[len(sent)])
        move.start()
        sent.append(move)

    lat = lax.axis_index("lat")
    core = lax.axis_index("core")
    gain = gain_ref[...]

    halves = []
    for half in range(2):
        src = lat if half == 0 else 1 - lat
        part = recv_ref[:, src].astype(F32)
        halves.append(part.reshape(256, LANES).astype(BF))
    for b in range(PSIDE):
        place = []
        pixels = []
        for half in range(2):
            place += [pmain_ref[half], prest_ref[half, b]]
            pixels += [halves[half][:, 256 * b : 256 * b + 256], halves[half][:, 1024:1152]]
        place = jnp.concatenate(place, axis=1)
        pixels = jnp.concatenate(pixels, axis=1)
        a_s[:, 256 * b : 256 * b + 256] = dot(place, pixels, NT).astype(BF)
        at_s[256 * b : 256 * b + 256, :] = dot(pixels, place, NT).astype(BF)
    moves[0].wait()
    for level in range(LEVELS):
        tok = dot(a_s[...], lw_ref[:, level * D : level * D + D]).astype(BF).astype(F32)
        for w in range(WINDOWS):
            t_s[w * WTOK + level * 72 : w * WTOK + level * 72 + 72, :] = tok[w * 72 : w * 72 + 72]

    bo_s[...] = t_s[...].astype(BF)
    send(bo_s, tok_far)

    def norm_step(w, carry):
        rows = pl.ds(pl.multiple_of(w * WTOK, WTOK), WTOK)
        x = t_s[rows, :]
        centred = x - jnp.mean(x, axis=-1, keepdims=True)
        inv = lax.rsqrt(jnp.mean(centred * centred, axis=-1, keepdims=True) + EPS)
        unit = centred * inv
        unit_s[rows, :] = unit
        inv_s[rows, :] = inv
        norm_s[rows, :] = (unit * gain).astype(BF)
        return carry

    lax.fori_loop(0, WINDOWS, norm_step, 0, unroll=True)
    moves[1].wait()
    for n in range(3):
        qkv_s[:, n * D : n * D + D] = dot(norm_s[...], wqkv_ref[:, n * D : n * D + D]).astype(BF)

    for move in moves[2:]:
        move.wait()
    low = lax.broadcasted_iota(jnp.int32, (1, 128), 1) < HDIM
    lane = lax.broadcasted_iota(jnp.int32, (1, 256), 1) // HDIM
    keep = [jnp.where(lane == e, 1.0, 0.0).astype(BF) for e in range(4)]

    def by_head(x):
        return jnp.concatenate([x * keep[e] for e in range(4)], axis=0)

    def own_heads(x):
        left = jnp.where(low, x[:WTOK, :128], x[WTOK : 2 * WTOK, :128])
        right = jnp.where(low, x[2 * WTOK : 3 * WTOK, 128:], x[3 * WTOK :, 128:])
        return jnp.concatenate([left, right], axis=1).astype(BF)

    def window_step(w, carry):
        rows = pl.ds(pl.multiple_of(w * WTOK, WTOK), WTOK)
        same = mcol_ref[w] == mrow_ref[w]
        state = []
        for part in range(2):
            at = part * 256
            keys = qkv_s[rows, D + at : D + at + 256]
            values = qkv_s[rows, 2 * D + at : 2 * D + at + 256]
            queries = by_head(qkv_s[rows, at : at + 256] * 0.125)
            grads = by_head(ga_ref[rows, at : at + 256])
            state.append((keys, values, queries, grads, dot(keys, queries, NT), dot(values, grads, NT)))
        ready = []
        for keys, values, queries, grads, score, gprob in state:
            score = jnp.where(same, score, -1e30)
            ex = jnp.exp(score - jnp.max(score, axis=0, keepdims=True))
            prob = ex * (1.0 / jnp.sum(ex, axis=0, keepdims=True))
            centred = gprob - jnp.sum(prob * gprob, axis=0, keepdims=True)
            ready.append(((prob * centred).astype(BF), prob.astype(BF)))
        for part in range(2):
            at = part * 256
            keys, values, queries, grads = state[part][:4]
            gscore, prob = ready[part]
            att_s[rows, at : at + 256] = own_heads(dot(prob, values, TN))
            gp_s[rows, at : at + 256] = own_heads(dot(gscore, keys * 0.125, TN))
            gp_s[rows, D + at : D + at + 256] = dot(gscore, queries).astype(BF)
            gp_s[rows, 2 * D + at : 2 * D + at + 256] = dot(prob, grads).astype(BF)
        return carry

    lax.fori_loop(0, WINDOWS, window_step, 0, unroll=True)

    send(att_s, att_far)

    total = dot(norm_s[...], gp_s[...], TN)
    for part in range(2):
        g_ref[core ^ part, :, 0:768] = total[:, 768 * part : 768 * part + 768].astype(BF)
    total = dot(att_s[...], gb_ref[...], TN)
    for part in range(2):
        g_ref[core ^ part, :, 768:1024] = total[:, 256 * part : 256 * part + 256].astype(BF)
    for i, target in enumerate((gown_far, goth_far)):
        send(g_ref.at[i, :, :1024], target.at[:, :1024])

    for part in range(2):
        rows = slice(part * PATCHES, part * PATCHES + PATCHES)
        h = dot(gp_s[rows, :], wqkv_ref[...], NT) * gain
        unit = unit_s[rows, :]
        shifted = inv_s[rows, :] * (
            h
            - jnp.mean(h, axis=-1, keepdims=True)
            - unit * jnp.mean(h * unit, axis=-1, keepdims=True)
        )
        total = (gb_ref[rows, :].astype(F32) + shifted.astype(BF).astype(F32)).astype(BF).astype(F32)
        for i in range(WINDOWS // 2):
            w = part * (WINDOWS // 2) + i
            for level in range(LEVELS):
                at = i * WTOK + level * 72
                gt_s[level, w * 72 : w * 72 + 72, :] = total[at : at + 72]

    grads = [gt_s[level].astype(BF) for level in range(LEVELS)]
    for b in range(PSIDE):
        slot = None
        for level in range(LEVELS):
            part = dot(at_s[256 * b : 256 * b + 256, :], grads[level])
            part = part * mix_ref[:, level : level + 1]
            slot = part if slot is None else slot + part
        gs_s[256 * b : 256 * b + 256, :] = slot.astype(BF)
    row = lax.broadcasted_iota(jnp.int32, (512, 1024), 0)
    idx = idxr_ref[...]
    for i, target in ((1, goth_far), (0, gown_far)):
        pick = jnp.where(row + 512 * i == idx, 1.0, 0.0).astype(BF)
        g_ref[i, :, 1024:1536] = dot(pick, gs_s[...]).astype(BF)
        send(g_ref.at[i, :, 1024:], target.at[:, 1024:])
    for move in sent:
        move.wait()


def out_kernel(tok_ref, att_ref, wproj_ref, tokt_ref, top_ref, bot_ref, side_top_ref, side_bot_ref):
    branch = dot(att_ref[...], wproj_ref[...]).astype(BF).astype(F32)
    total = (tok_ref[...].astype(F32) + branch).astype(BF)
    top_ref[...] = dot(tokt_ref[:PATCHES], total).astype(BF)
    bot_ref[...] = dot(tokt_ref[PATCHES:TOKENS], total).astype(BF)
    sides = dot(tokt_ref[TOKENS:], total).astype(BF)
    side_top_ref[...] = sides[:STRIP]
    side_bot_ref[...] = sides[STRIP : 2 * STRIP]


def add_kernel(left_ref, right_ref, out_ref):
    out_ref[...] = (left_ref[...] + right_ref[...].astype(F32)).astype(BF)


def join_half(part, ref, qkv_far, proj_far, qkv_s, proj_s, sems):
    moves = []
    for near, far, first in ((qkv_s, qkv_far, 0), (proj_s, proj_far, 768)):
        width = near.shape[1]
        near[...] = ref[:, first : first + width].astype(F32)
        at = pl.multiple_of((lax.axis_index("core") ^ part) * width, 256)
        move = pltpu.make_async_copy(near, far.at[:, pl.ds(at, width)], sems.at[len(moves)])
        move.start()
        moves.append(move)
    for move in moves:
        move.wait()


def own_kernel(mine_ref, *rest):
    join_half(0, mine_ref, *rest)


def other_kernel(other_ref, qkv_in, proj_in, *rest):
    join_half(1, other_ref, *rest)


def shape(*dims, dtype=BF):
    return jax.ShapeDtypeStruct(dims, dtype)


def cost(us):
    return pl.CostEstimate(flops=int(us * 1e9), bytes_accessed=0, transcendentals=0)


def vmem_call(kernel, outs, scratch=(), count=0, far=(), far_out=(), mib=58, us=1, aliases=None):
    def spec(is_far):
        return pl.BlockSpec(memory_space=pl.ANY if is_far else pltpu.VMEM)

    many = isinstance(outs, (list, tuple))
    return pl.pallas_call(
        kernel,
        out_shape=outs,
        in_specs=[spec(i in far) for i in range(count)],
        out_specs=[spec(i in far_out) for i in range(len(outs))] if many else spec(False),
        scratch_shapes=list(scratch),
        input_output_aliases=aliases or {},
        compiler_params=pltpu.CompilerParams(vmem_limit_bytes=mib * 1024 * 1024),
        cost_estimate=cost(us),
    )


def per_device(
    counts,
    pixels,
    var_order,
    embed_weight,
    level_mix,
    norm_gain,
    w_qkv,
    w_proj,
    mask_ids,
    cotangent,
):
    chips, lats, lons = counts
    bands = chips * 2
    lat = lax.axis_index("lat")
    core = lax.axis_index("core")
    lon = lax.axis_index("lon")
    rows_ring = ("chip", "core", "lat")
    everyone = ("chip", "core", "lat", "lon")
    ring = bands * lats
    group = ("chip", "lat", "lon")
    group_size = chips * lats * lons

    swap_lon = [(0, 1), (1, 0)]
    swap_core = [(0, 1), (1, 0)]

    main, edge = pixel_place()
    border, ahead, corner, copies = vmem_call(
        edge_kernel,
        [
            shape(2 * bands * 8 + 4 * STRIP, 128),
            shape(HALF, LEVELS, COLS, D),
            shape(STRIP, D),
            shape(chips, 32, D),
        ],
        count=5,
        us=3,
    )(
        pixels,
        cotangent,
        embed_weight.reshape(32, D),
        jnp.asarray(edge_place(), BF),
        jnp.asarray(strip_place(), BF),
    )
    halo = lax.ppermute(border, "lon", swap_lon)
    halo, ahead, corner = lax.optimization_barrier((halo, ahead, corner))
    ahead = lax.ppermute(ahead, rows_ring, [(i, (i - 1) % ring) for i in range(ring)])
    corner = lax.ppermute(
        corner,
        everyone,
        [(i * 2 + k, ((i - 1) % ring) * 2 + 1 - k) for i in range(ring) for k in range(2)],
    )
    own_weight = lax.all_to_all(copies, "chip", split_axis=0, concat_axis=0, tiled=True)
    own_weight = own_weight.reshape(512, D)
    oth_weight = lax.ppermute(own_weight, "core", swap_core)

    (packed,) = vmem_call(
        pack_kernel,
        [shape(bands, 2, 8, LANES)],
        [
            pltpu.VMEM((2, bands * 8, LANES), BF),
            pltpu.VMEM((LANES, LANES), BF),
            pltpu.VMEM((2, bands, 8, LANES), BF),
            pltpu.SemaphoreType.DMA((3,)),
        ],
        count=4,
        far=(3,),
        far_out=(0,),
        us=6,
    )(pixels, jnp.asarray(edge, BF), halo, jnp.asarray(main, BF))
    recv = lax.all_to_all(
        packed.reshape(bands * 2, 8, LANES), rows_ring, split_axis=0, concat_axis=0, tiled=True
    ).reshape(bands, 2, 8, LANES)

    var_order, ahead, corner = lax.optimization_barrier((var_order, ahead, corner))
    device = var_order // 2
    base = jnp.where(device % 2 == core, 0, 512) + (device // 2) * 32 + (var_order % 2) * 16
    index = base[None, :, None] + (
        jnp.arange(4)[:, None, None] + 4 * jnp.arange(4)[None, None, :]
    )
    index = index.reshape(1024).astype(jnp.int32)
    slot_mix = jnp.repeat(level_mix[var_order], 4, axis=0)

    ids = mask_ids.reshape(2, HALF, LEVELS, WINDOWS, WCOL).transpose(3, 2, 0, 1, 4)
    ids = ids.reshape(WINDOWS, WTOK)

    tok = token_place()
    level_weight, grad_branch, grad_attended = vmem_call(
        prepare_kernel, [shape(1024, 1024), shape(TOKENS, D), shape(TOKENS, D)], count=10, us=8
    )(
        index[:, None],
        slot_mix,
        own_weight,
        oth_weight,
        cotangent,
        ahead,
        halo,
        corner,
        jnp.asarray(tok, BF),
        w_proj,
    )

    pmain, prest = patch_place()
    tokens, attended, gown, goth = vmem_call(
        block_kernel,
        [
            shape(TOKENS, D),
            shape(TOKENS, D),
            shape(512, 1536),
            shape(512, 1536),
        ],
        [
            pltpu.VMEM((1024, 1024), BF),
            pltpu.VMEM((D, 3 * D), BF),
            pltpu.VMEM((TOKENS, D), BF),
            pltpu.VMEM((TOKENS, D), BF),
            pltpu.VMEM((2, 512, 1536), BF),
            pltpu.VMEM((PATCHES, 1024), BF),
            pltpu.VMEM((1024, PATCHES), BF),
            pltpu.VMEM((TOKENS, D), F32),
            pltpu.VMEM((TOKENS, D), F32),
            pltpu.VMEM((TOKENS, 1), F32),
            pltpu.VMEM((TOKENS, D), BF),
            pltpu.VMEM((TOKENS, 3 * D), BF),
            pltpu.VMEM((TOKENS, D), BF),
            pltpu.VMEM((TOKENS, 3 * D), BF),
            pltpu.VMEM((TOKENS, D), BF),
            pltpu.VMEM((LEVELS, PATCHES, D), F32),
            pltpu.VMEM((1024, D), BF),
            pltpu.SemaphoreType.DMA((4,)),
            pltpu.SemaphoreType.DMA((6,)),
        ],
        count=12,
        far=range(8, 12),
        far_out=(0, 1, 2, 3),
        us=28,
    )(
        recv,
        index[None, :],
        slot_mix,
        norm_gain[None, :],
        ids[:, :, None],
        jnp.tile(ids, (1, 4))[:, None, :],
        jnp.asarray(pmain, BF),
        jnp.asarray(prest, BF),
        level_weight,
        w_qkv,
        grad_branch,
        grad_attended,
    )

    from_core = lax.ppermute(goth, "core", swap_core)
    wide = gown.astype(F32)
    chip_sum = vmem_call(add_kernel, shape(512, 1536), count=2, mib=12, us=2)(wide, from_core)
    terms = lax.all_to_all(
        chip_sum.reshape(group_size, 8, 1536), group, split_axis=0, concat_axis=0, tiled=True
    )
    owned = jnp.sum(terms.astype(F32), axis=0).astype(BF)
    copies = jnp.broadcast_to(owned[None, :, :1024], (group_size, 8, 1024))
    mine = lax.all_to_all(copies, group, split_axis=0, concat_axis=0, tiled=True)
    mine = mine.reshape(512, 1024)

    embed_part = owned[:, 1024:]
    pieces = [embed_part]
    for dlat, dlon in ((0, 1), (1, 0), (1, 1)):
        pieces.append(
            lax.ppermute(
                embed_part,
                ("lat", "lon"),
                [(i * 2 + k, (i ^ dlat) * 2 + (k ^ dlon)) for i in range(2) for k in range(2)],
            )
        )
    stacked = jnp.stack(pieces)
    tile = lat * 2 + lon
    grad_embed = jnp.concatenate(
        [lax.dynamic_index_in_dim(stacked, tile ^ t, 0, keepdims=False) for t in range(4)], axis=0
    )
    grad_embed = grad_embed.reshape(2, 16, D).astype(F32)

    top, bot, side_top, side_bot = vmem_call(
        out_kernel,
        [shape(PATCHES, D), shape(PATCHES, D), shape(STRIP, D), shape(STRIP, D)],
        count=4,
        us=5,
    )(tokens, attended, w_proj, jnp.asarray(tok.T, BF))
    from_before = lax.ppermute(bot, rows_ring, [(i, (i + 1) % ring) for i in range(ring)])
    west = lax.ppermute(side_top, "lon", swap_lon)
    south_west = lax.ppermute(
        side_bot,
        everyone,
        [(i * 2 + k, ((i + 1) % ring) * 2 + 1 - k) for i in range(ring) for k in range(2)],
    )
    _, from_before, west, south_west = lax.optimization_barrier((owned, from_before, west, south_west))
    body = jnp.concatenate([from_before, top], axis=0).reshape(ROWS, LEVELS, COLS, D)
    sides = jnp.concatenate([south_west[:36], west[:36]], axis=0).reshape(ROWS, LEVELS, 3, D)
    block_out = jnp.concatenate([sides, body[:, :, 3:]], axis=2)

    mine, block_out, grad_embed = lax.optimization_barrier((mine, block_out, grad_embed))
    other = lax.ppermute(mine, "core", swap_core)
    full = [shape(512, 1536, dtype=F32), shape(512, 512, dtype=F32)]
    room = [
        pltpu.VMEM((512, 768), F32),
        pltpu.VMEM((512, 256), F32),
        pltpu.SemaphoreType.DMA((2,)),
    ]
    own = vmem_call(own_kernel, full, room, count=1, far_out=(0, 1), mib=10, us=2)(mine)
    grad_qkv, grad_proj = vmem_call(
        other_kernel, full, room, 3, (1, 2), (0, 1), mib=10, us=2, aliases={1: 0, 2: 1}
    )(other, *own)
    return (block_out, grad_embed, grad_qkv, grad_proj)


def solution(mesh):
    var, lats, lons = (mesh.shape[name] for name in ("var", "lat", "lon"))
    chips = var // 2
    fine = Mesh(mesh.devices.reshape(chips, 2, lats, lons), ("chip", "core", "lat", "lon"))
    both = ("chip", "core")
    in_specs = (
        P(None, "lat", both, None, "lon"),
        P(),
        P(both, None, None),
        P(),
        P(),
        P(),
        P(),
        P(("chip", "core", "lat"), None, "lon"),
        P(("chip", "core", "lat"), None, "lon", None),
    )
    out_specs = (P(("chip", "core", "lat"), None, "lon", None), P(both, None, None), P(), P())
    return jax.shard_map(
        functools.partial(per_device, (chips, lats, lons)),
        mesh=fine,
        in_specs=in_specs,
        out_specs=out_specs,
        check_vma=False,
    )
```
